32 devices in a mesh: row: 4 (over z), ma: 8 (over y, x, core).
Axes of the slice: x: 2, y: 2, z: 4, core: 2. Of those that a mesh axis runs over, the one named last changes fastest.
Arguments:
- toroidal_stream_spectra: float32 [2, 4, 512, 512], P(None, 'row', 'ma'), may hold values from -6 to 6, as said below
- thermal_spectra: float32 [2, 4, 512, 512], P(None, 'row', 'ma'), may hold values from -6 to 6, as said below
- induction_potential: float32 [2, 4, 512, 512], P(None, 'row', 'ma'), may hold values from -6 to 6, as said below
- outward_speed_spectra: float32 [2, 4, 512, 512], P(None, 'row', 'ma'), may hold values from -60 to 60, as said below
- position_azimuth_map: int32 [512], replicated, may hold values from 0 to 511, as said below
- subdiagonal_complement: float32 [2, 4, 512], P(None, 'row'), may hold values from 0.005 to 0.3
- superdiagonal_complement: float32 [2, 4, 512], P(None, 'row'), may hold values from 0.005 to 0.3
- diagonal_entries: float32 [2, 4, 512], P(None, 'row'), may hold values from 2 to 16
Outputs:
- new_temperature: float32 [2, 4, 512, 512], P(None, 'row', 'ma')
- new_magnetic: float32 [2, 4, 512, 512], P(None, 'row', 'ma')
The draws below stay inside these ranges and needn't reach their ends.
Inputs may be any that keep to these rules, and one draw needn't show every extreme that they name: `position_azimuth_map`: slots 2 i and 2 i + 1 hold the orders m and 511 - m; every order stands in exactly one slot. `toroidal_stream_spectra`: an entry whose degree is below the order of its slot in position_azimuth_map is zero. `thermal_spectra`: an entry whose degree is below the order of its slot in position_azimuth_map is zero. `induction_potential`: an entry whose degree is below the order of its slot in position_azimuth_map is zero. `outward_speed_spectra`: an entry whose degree is below the order of its slot in position_azimuth_map is zero.
All inputs are finite; a program needn't handle non-finite values.
Results may differ from the reference program's by a relative error of at most 0.00035.
Values sent between devices are 32-bit elements; how exact they have to be, the bound alone decides.
A program may use at most 128 MiB of HBM per device.

```python
import math
import jax
import jax.numpy as jnp
from jax import lax

DEGREES = 512
NLAT = 768
NLON = 1536
SHELLS = 4


def slot_orders(key):
    pair_low = jax.random.permutation(jax.random.fold_in(key, 11), DEGREES // 2).astype(jnp.int32)
    partner = DEGREES - 1 - pair_low
    return jnp.stack([pair_low, partner], axis=1).reshape(DEGREES)


def spectrum(key, salt_code, strength):
    orders = slot_orders(key)
    degree_vals = jnp.arange(DEGREES, dtype=jnp.float32)
    live_mask = (degree_vals[None, :] >= orders.astype(jnp.float32)[:, None]).astype(jnp.float32)
    decay_rows = strength / ((1.0 + degree_vals) * jnp.sqrt(1.0 + degree_vals))
    array_shape = (2, SHELLS, DEGREES, DEGREES)
    noise_key = jax.random.fold_in(key, salt_code)
    values = jnp.clip(jax.random.normal(noise_key, array_shape, jnp.float32), -6.0, 6.0)
    return values * decay_rows * live_mask


def draw_position_azimuth_map(key, part):
    return slot_orders(key)


def draw_toroidal_stream_spectra(key, part):
    return spectrum(key, 21, 1.0)


def draw_thermal_spectra(key, part):
    return spectrum(key, 22, 1.0)


def draw_induction_potential(key, part):
    return spectrum(key, 23, 1.0)


def draw_outward_speed_spectra(key, part):
    return spectrum(key, 24, 10.0)


def block_levels(key, extent, shards, low, largest):
    level, own = 1.0, jax.random.fold_in(key, 6)
    for dim, parts in shards:
        heights = jnp.exp(jax.random.uniform(jax.random.fold_in(own, dim), (parts,), jnp.float32, low / len(shards), largest / len(shards)))
        level = level * jnp.repeat(heights, extent[dim] // parts).reshape([-1 if axis == dim else 1 for axis in range(len(extent))])
    return level


def setup_inputs(seed: int = 0) -> dict:
    keys = jax.random.split(jax.random.key(seed), 9)
    toroidal_stream_spectra = draw_toroidal_stream_spectra(jax.random.fold_in(keys[8], 71), 0)
    thermal_spectra = draw_thermal_spectra(jax.random.fold_in(keys[8], 71), 0)
    induction_potential = draw_induction_potential(jax.random.fold_in(keys[8], 71), 0)
    outward_speed_spectra = draw_outward_speed_spectra(jax.random.fold_in(keys[8], 71), 0)
    position_azimuth_map = draw_position_azimuth_map(jax.random.fold_in(keys[8], 71), 0)
    subdiagonal_complement = jnp.clip(jnp.exp(math.log(0.3) - 4.0943446 * jax.random.uniform(keys[5], (2, SHELLS, DEGREES), jnp.float32) ** block_levels(keys[5], (2, SHELLS, DEGREES), ((1, 4),), -0.2, 0.2)), 0.005, 0.3)
    superdiagonal_complement = jnp.clip(jnp.exp(math.log(0.3) - 4.0943446 * jax.random.uniform(keys[6], (2, SHELLS, DEGREES), jnp.float32) ** block_levels(keys[6], (2, SHELLS, DEGREES), ((1, 4),), -0.2, 0.2)), 0.005, 0.3)
    diagonal_entries = jnp.clip(jnp.exp(math.log(16.0) - 2.0794415 * jax.random.uniform(keys[7], (2, SHELLS, DEGREES), jnp.float32) ** block_levels(keys[7], (2, SHELLS, DEGREES), ((1, 4),), -0.2, 0.2)), 2.0, 16.0)
    return dict(toroidal_stream_spectra=toroidal_stream_spectra, thermal_spectra=thermal_spectra, induction_potential=induction_potential, outward_speed_spectra=outward_speed_spectra, position_azimuth_map=position_azimuth_map, subdiagonal_complement=subdiagonal_complement, superdiagonal_complement=superdiagonal_complement, diagonal_entries=diagonal_entries)


inner_radius = 0.35
shell_span = 0.65
time_step = 0.001
highest = lax.Precision.HIGHEST
log_gamma_half = 0.5 * math.log(math.pi) - math.log(2.0)

def legendre_rows(orders, cosine, sine_vals, harmonic_index_array):
    block_len = math.gcd(32, harmonic_index_array)
    dtype_ref = cosine.dtype
    order_col = orders.astype(dtype_ref)[:, None]
    log_start = 0.5 * (lax.lgamma(order_col + 1.5) - lax.lgamma(order_col + 1.0) - log_gamma_half) - 0.5 * math.log(2.0) + order_col * jnp.log(sine_vals)[None, :]
    zero_state = jnp.zeros(log_start.shape, dtype_ref)
    legendre = jnp.zeros((orders.shape[0], harmonic_index_array, cosine.shape[0]), dtype_ref)

    def sweep(position, state_tuple):
        before, current, log_scale, legendre = state_tuple
        new_rows = []
        for offset in range(block_len):
            degree_now = (position * block_len + offset).astype(dtype_ref)
            above_diag = degree_now > order_col
            square = degree_now * degree_now - order_col * order_col
            denominator = jnp.where(above_diag, square, 1.0)
            rise_coef = jnp.where(above_diag, jnp.sqrt(jnp.maximum(4.0 * degree_now * degree_now - 1.0, 1.0) / denominator), 0.0)
            lower_term = (degree_now - 1.0) * (degree_now - 1.0) - order_col * order_col
            fall_coef = jnp.where(above_diag, jnp.sqrt(jnp.maximum((2.0 * degree_now + 1.0) * lower_term, 0.0) / (jnp.maximum(2.0 * degree_now - 3.0, 1.0) * denominator)), 0.0)
            fresh_row = jnp.where(degree_now == order_col, 1.0, rise_coef * cosine[None, :] * current - fall_coef * before)
            before, current = (current, fresh_row)
            new_rows.append(fresh_row * jnp.exp(log_scale))
        magnitude = jnp.maximum(jnp.abs(before), jnp.abs(current))
        magnitude = jnp.where(magnitude > 0.0, magnitude, 1.0)
        before = before / magnitude
        current = current / magnitude
        log_scale = log_scale + jnp.log(magnitude)
        first_row = (position * block_len).astype(jnp.int32)
        legendre = lax.dynamic_update_slice(legendre, jnp.stack(new_rows, axis=1), (jnp.int32(0), first_row, jnp.int32(0)))
        return (before, current, log_scale, legendre)
    state_tuple = lax.fori_loop(0, harmonic_index_array // block_len, sweep, (zero_state, zero_state, log_start, legendre))
    return state_tuple[3]

def wave_table(orders, first_col, column_count, lon_total):
    column_ids = first_col + jnp.arange(column_count, dtype=jnp.int32)
    phase_int = orders[:, None] * column_ids[None, :] % lon_total
    angle_vals = 2.0 * math.pi / lon_total * phase_int.astype(jnp.float32)
    return jnp.stack([jnp.cos(angle_vals), -jnp.sin(angle_vals)], axis=1)

def to_longitudes(spectra, orders, lon_total):
    order_weight = jnp.where(orders == 0, 1.0, 2.0).astype(spectra.dtype)
    weighted = spectra * order_weight[:, None, None, None, None]
    lon_block = math.gcd(512, lon_total)
    output_buf = jnp.zeros((spectra.shape[1], spectra.shape[2], spectra.shape[4], lon_total), spectra.dtype)

    def place(position, output_buf):
        first_col = (position * lon_block).astype(jnp.int32)
        wave_block = wave_table(orders, first_col, lon_block, lon_total).astype(spectra.dtype)
        grid_piece = jnp.einsum('mfscn,mcp->fsnp', weighted, wave_block, precision=highest)
        return lax.dynamic_update_slice(output_buf, grid_piece, (jnp.int32(0), jnp.int32(0), jnp.int32(0), first_col))
    return lax.fori_loop(0, lon_total // lon_block, place, output_buf)

def from_longitudes(grid_sets, orders, lon_total):
    lon_block = math.gcd(512, lon_total)
    running_sum = jnp.zeros((orders.shape[0], grid_sets.shape[0], grid_sets.shape[1], 2, grid_sets.shape[2]), grid_sets.dtype)

    def add_block(position, running_sum):
        first_col = (position * lon_block).astype(jnp.int32)
        wave_block = wave_table(orders, first_col, lon_block, lon_total).astype(grid_sets.dtype)
        grid_piece = lax.dynamic_slice_in_dim(grid_sets, first_col, lon_block, 3)
        return running_sum + jnp.einsum('fsnp,mcp->mfscn', grid_piece, wave_block, precision=highest)
    return lax.fori_loop(0, lon_total // lon_block, add_block, running_sum) / lon_total

def fejer_weights(node_count, lat_total):
    term_count = lat_total // 2
    wave_ints = jnp.arange(1, term_count + 1, dtype=jnp.int32)
    node_ints = 2 * jnp.arange(node_count, dtype=jnp.int32) + 1
    phase_int = wave_ints[:, None] * node_ints[None, :] % (2 * lat_total)
    cosines = jnp.cos(math.pi / lat_total * phase_int.astype(jnp.float32))
    wave_vals = wave_ints.astype(jnp.float32)
    ratio_vals = cosines / (4.0 * wave_vals * wave_vals - 1.0)[:, None]
    return 2.0 / lat_total * (1.0 - 2.0 * lax.optimization_barrier(jnp.sum(ratio_vals, axis=0)))

def nonlinear(grid_sets, factor):
    heat_term = -((grid_sets[3] * grid_sets[1] - grid_sets[0] * grid_sets[4]) * factor + grid_sets[6] * grid_sets[7])
    field_term = -((grid_sets[3] * grid_sets[2] - grid_sets[0] * grid_sets[5]) * factor + grid_sets[6] * grid_sets[8])
    return jnp.stack([heat_term, field_term])

def reference(toroidal_stream_spectra, thermal_spectra, induction_potential, outward_speed_spectra, position_azimuth_map, subdiagonal_complement, superdiagonal_complement, diagonal_entries):
    layer_indices = thermal_spectra.shape[1]
    harmonic_index_array = thermal_spectra.shape[3]
    spacing = shell_span / layer_indices
    order_group = math.gcd(16, harmonic_index_array)
    block_total = harmonic_index_array // order_group
    degree_vals = jnp.arange(harmonic_index_array, dtype=jnp.float32)
    theta_all = math.pi * (jnp.arange(NLAT, dtype=jnp.float32) + 0.5) / NLAT
    cosine_all = jnp.cos(theta_all)
    sine_all = jnp.sin(theta_all)
    order_float = position_azimuth_map.astype(jnp.float32)
    above_diag = degree_vals[None, :] > order_float[:, None]
    link_coef = jnp.where(above_diag, jnp.sqrt(jnp.maximum((2.0 * degree_vals + 1.0) * (degree_vals * degree_vals - order_float[:, None] * order_float[:, None]), 0.0) / jnp.maximum(2.0 * degree_vals - 1.0, 1.0)), 0.0)
    coupled_quantities = jnp.stack([thermal_spectra, induction_potential])
    padded = jnp.pad(coupled_quantities, ((0, 0), (0, 0), (1, 1), (0, 0), (0, 0)))
    depthwise_slope = (padded[:, :, 2:] - padded[:, :, :-2]) / (2.0 * spacing)
    entire_arguments = jnp.stack([toroidal_stream_spectra, thermal_spectra, induction_potential, outward_speed_spectra, depthwise_slope[0], depthwise_slope[1]])

    def synth_block(position):
        first_row = (position * order_group).astype(jnp.int32)
        coef_block = lax.dynamic_slice_in_dim(entire_arguments, first_row, order_group, 3)
        link_block = lax.dynamic_slice_in_dim(link_coef, first_row, order_group, 0)
        orders_block = lax.dynamic_slice_in_dim(order_float, first_row, order_group, 0)
        motion_groupings = coef_block[:3]
        weighted = motion_groupings * degree_vals
        product = motion_groupings * link_block[None, None, None]
        lifted = jnp.concatenate([product[..., 1:], jnp.zeros_like(product[..., :1])], axis=-1)
        coef_sets = jnp.concatenate([motion_groupings, weighted, lifted, coef_block[3:]], axis=0)
        coeffs = jnp.transpose(coef_sets, (3, 0, 2, 1, 4)).reshape(order_group, 12 * layer_indices * 2, harmonic_index_array)
        legendre = legendre_rows(orders_block, cosine_all, sine_all, harmonic_index_array)
        result = jnp.einsum('ocl,oln->ocn', coeffs, legendre, precision=highest).reshape(order_group, 12, layer_indices, 2, NLAT)
        spin_rate = orders_block[:, None, None, None]
        plain_part = result[:, 0:3]
        turned = jnp.stack([-spin_rate * plain_part[:, :, :, 1], spin_rate * plain_part[:, :, :, 0]], axis=3)
        slant_part = cosine_all * result[:, 3:6] - result[:, 6:9]
        return jnp.concatenate([turned, slant_part, result[:, 9:12]], axis=1)
    synth = lax.map(synth_block, jnp.arange(block_total)).reshape(harmonic_index_array, 9, layer_indices, 2, NLAT)

    def shell_step(position):
        shell_now = position.astype(jnp.int32)
        spectra = lax.dynamic_slice_in_dim(synth, shell_now, 1, 2)
        grid_sets = to_longitudes(spectra, position_azimuth_map, NLON)
        radius = inner_radius + spacing * (shell_now.astype(jnp.float32) + 0.5)
        factor = 1.0 / (radius * radius * sine_all * sine_all)
        forcing = nonlinear(grid_sets, factor[None, :, None])
        return from_longitudes(forcing, position_azimuth_map, NLON)
    returned = lax.map(shell_step, jnp.arange(layer_indices))
    returned = jnp.transpose(returned[:, :, :, 0], (1, 2, 0, 3, 4))
    weights = fejer_weights(NLAT, NLAT)
    values = returned.reshape(harmonic_index_array, 4 * layer_indices, NLAT) * weights

    def analysis_block(position):
        first_row = (position * order_group).astype(jnp.int32)
        coef_block = lax.dynamic_slice_in_dim(values, first_row, order_group, 0)
        orders_block = lax.dynamic_slice_in_dim(order_float, first_row, order_group, 0)
        legendre = legendre_rows(orders_block, cosine_all, sine_all, harmonic_index_array)
        return jnp.einsum('ocn,oln->ocl', coef_block, legendre, precision=highest)
    tendency = lax.map(analysis_block, jnp.arange(block_total)).reshape(harmonic_index_array, 2, layer_indices, 2, harmonic_index_array)
    tendency = jnp.transpose(tendency, (1, 3, 2, 0, 4))
    right_side = coupled_quantities + time_step * tendency
    keep_low = 1.0 - subdiagonal_complement
    keep_up = 1.0 - superdiagonal_complement

    def forward(carry_val, shell_data):
        running = shell_data[0] + shell_data[1][:, None, None, :] * carry_val
        return (running, running / shell_data[2][:, None, None, :])
    zero_block = jnp.zeros((2, 2, harmonic_index_array, harmonic_index_array), right_side.dtype)
    last_state, scaled = lax.scan(forward, zero_block, (jnp.moveaxis(right_side, 2, 0), jnp.moveaxis(keep_low, 1, 0), jnp.moveaxis(diagonal_entries, 1, 0)))

    def backward(carry_val, shell_data):
        running = shell_data[0] + shell_data[1][:, None, None, :] * carry_val
        return (running, running)
    last_state, solved = lax.scan(backward, zero_block, (scaled, jnp.moveaxis(keep_up, 1, 0)), reverse=True)
    solved = jnp.moveaxis(solved, 0, 2)
    return (solved[0], solved[1])
```

```python
import functools
import math

import jax
import jax.numpy as jnp
from jax import lax
from jax.experimental import pallas as pl
from jax.experimental.pallas import tpu as pltpu
from jax.sharding import PartitionSpec as P

NLAT = 768
NLON = 1536


inner_radius = 0.35
shell_span = 0.65
time_step = 0.001
highest = lax.Precision.HIGHEST
log_gamma_half = 0.5 * math.log(math.pi) - math.log(2.0)


def extended(block, sides, width):
    for axis, dim in sides:
        count = lax.axis_size(axis)
        forward = [(i, i + 1) for i in range(count - 1)]
        backward = [(target, source) for source, target in forward]
        low = lax.ppermute(
            lax.slice_in_dim(block, block.shape[dim] - width, None, axis=dim), axis, forward
        )
        high = lax.ppermute(lax.slice_in_dim(block, 0, width, axis=dim), axis, backward)
        block = jnp.concatenate([low, block, high], axis=dim)
    return block


def entering_2(part, axis, combine, identity, reverse):
    count = lax.axis_size(axis)
    place = lax.axis_index(axis)
    ahead = count - 1 - place if reverse else place
    gathered = jax.tree.map(lambda a: lax.all_gather(a, axis), part)
    state = jax.tree.map(lambda a, e: jnp.zeros_like(a) + jnp.asarray(e, a.dtype), part, identity)

    def one(step, state):
        source = count - 1 - step if reverse else step
        return combine(
            state, jax.tree.map(lambda a: lax.dynamic_index_in_dim(a, source, 0, False), gathered)
        )

    return lax.fori_loop(0, ahead, one, state)


def legendre_rows(orders, cosine, sine_vals, harmonic_index_array):
    block_len = math.gcd(32, harmonic_index_array)
    dtype_ref = cosine.dtype
    order_col = orders[:, None]
    log_start = (
        0.5 * (lax.lgamma(order_col + 1.5) - lax.lgamma(order_col + 1.0) - log_gamma_half)
        - 0.5 * math.log(2.0)
        + order_col * jnp.log(sine_vals)[None, :]
    )
    zero_state = jnp.zeros(log_start.shape, dtype_ref)
    legendre = jnp.zeros((orders.shape[0], harmonic_index_array, cosine.shape[0]), dtype_ref)

    def sweep(position, state_tuple):
        before, current, log_scale, legendre = state_tuple
        new_rows = []
        for offset in range(block_len):
            degree_now = (position * block_len + offset).astype(dtype_ref)
            above_diag = degree_now > order_col
            square = degree_now * degree_now - order_col * order_col
            denominator = jnp.where(above_diag, square, 1.0)
            rise_coef = jnp.where(
                above_diag,
                jnp.sqrt(jnp.maximum(4.0 * degree_now * degree_now - 1.0, 1.0) / denominator),
                0.0,
            )
            lower_term = (degree_now - 1.0) * (degree_now - 1.0) - order_col * order_col
            fall_coef = jnp.where(
                above_diag,
                jnp.sqrt(
                    jnp.maximum((2.0 * degree_now + 1.0) * lower_term, 0.0)
                    / (jnp.maximum(2.0 * degree_now - 3.0, 1.0) * denominator)
                ),
                0.0,
            )
            fresh_row = jnp.where(
                degree_now == order_col,
                1.0,
                rise_coef * cosine[None, :] * current - fall_coef * before,
            )
            before, current = (current, fresh_row)
            new_rows.append(fresh_row * jnp.exp(log_scale))
        magnitude = jnp.maximum(jnp.abs(before), jnp.abs(current))
        magnitude = jnp.where(magnitude > 0.0, magnitude, 1.0)
        before = before / magnitude
        current = current / magnitude
        log_scale = log_scale + jnp.log(magnitude)
        first_row = (position * block_len).astype(jnp.int32)
        legendre = lax.dynamic_update_slice(
            legendre, jnp.stack(new_rows, axis=1), (jnp.int32(0), first_row, jnp.int32(0))
        )
        return (before, current, log_scale, legendre)

    state_tuple = lax.fori_loop(
        0, harmonic_index_array // block_len, sweep, (zero_state, zero_state, log_start, legendre)
    )
    return state_tuple[3]


def wave_table(orders, first_col, column_count, lon_total):
    column_ids = first_col + jnp.arange(column_count, dtype=jnp.int32)
    phase_int = orders[:, None] * column_ids[None, :] % lon_total
    angle_vals = 2.0 * math.pi / lon_total * phase_int.astype(jnp.float32)
    return jnp.stack([jnp.cos(angle_vals), -jnp.sin(angle_vals)], axis=1)


def to_longitudes(spectra, orders, lon_total):
    order_weight = jnp.where(orders == 0, 1.0, 2.0).astype(spectra.dtype)
    weighted = spectra * order_weight[:, None, None, None, None]
    lon_block = math.gcd(512, lon_total)
    output_buf = jnp.zeros(
        (spectra.shape[1], spectra.shape[2], spectra.shape[4], lon_total), spectra.dtype
    )

    def place(position, output_buf):
        first_col = (position * lon_block).astype(jnp.int32)
        wave_block = wave_table(orders, first_col, lon_block, lon_total)
        grid_piece = jnp.einsum("mfscn,mcp->fsnp", weighted, wave_block, precision=highest)
        return lax.dynamic_update_slice(
            output_buf, grid_piece, (jnp.int32(0), jnp.int32(0), jnp.int32(0), first_col)
        )

    return lax.fori_loop(0, lon_total // lon_block, place, output_buf)


def from_longitudes(grid_sets, orders, lon_total):
    lon_block = math.gcd(512, lon_total)
    running_sum = jnp.zeros(
        (orders.shape[0], grid_sets.shape[0], grid_sets.shape[1], 2, grid_sets.shape[2]),
        grid_sets.dtype,
    )

    def add_block(position, running_sum):
        first_col = (position * lon_block).astype(jnp.int32)
        wave_block = wave_table(orders, first_col, lon_block, lon_total)
        grid_piece = lax.dynamic_slice_in_dim(grid_sets, first_col, lon_block, 3)
        return running_sum + jnp.einsum(
            "fsnp,mcp->mfscn", grid_piece, wave_block, precision=highest
        )

    return lax.fori_loop(0, lon_total // lon_block, add_block, running_sum) / lon_total


def fejer_weights(node_count, lat_total):
    term_count = lat_total // 2
    wave_ints = jnp.arange(1, term_count + 1, dtype=jnp.int32)
    node_ints = 2 * jnp.arange(node_count, dtype=jnp.int32) + 1
    phase_int = wave_ints[:, None] * node_ints[None, :] % (2 * lat_total)
    cosines = jnp.cos(math.pi / lat_total * phase_int.astype(jnp.float32))
    wave_vals = wave_ints.astype(jnp.float32)
    ratio_vals = cosines / (4.0 * wave_vals * wave_vals - 1.0)[:, None]
    return 2.0 / lat_total * (1.0 - 2.0 * jnp.sum(ratio_vals, axis=0))


def nonlinear(grid_sets, factor):
    heat_term = -(
        (grid_sets[3] * grid_sets[1] - grid_sets[0] * grid_sets[4]) * factor
        + grid_sets[6] * grid_sets[7]
    )
    field_term = -(
        (grid_sets[3] * grid_sets[2] - grid_sets[0] * grid_sets[5]) * factor
        + grid_sets[6] * grid_sets[8]
    )
    return jnp.stack([heat_term, field_term])


def join_maps(earlier_map, later_map):
    return (
        earlier_map[0] * later_map[0],
        earlier_map[1] * later_map[0][:, None, None, :] + later_map[1],
    )


def body(
    toroidal_stream_spectra,
    thermal_spectra,
    induction_potential,
    outward_speed_spectra,
    position_azimuth_map,
    subdiagonal_complement,
    superdiagonal_complement,
    diagonal_entries,
):
    layer_indices = thermal_spectra.shape[1]
    local_azimuthal_numbers = thermal_spectra.shape[2]
    harmonic_index_array = thermal_spectra.shape[3]
    latitude_rows = NLAT // lax.axis_size("ma")
    north_count = NLAT // 2
    spacing = shell_span / (layer_indices * lax.axis_size("row"))
    slot_start = lax.axis_index("ma") * local_azimuthal_numbers
    my_orders = lax.dynamic_slice_in_dim(position_azimuth_map, slot_start, local_azimuthal_numbers)
    order_float = my_orders.astype(jnp.float32)
    degree_vals = jnp.arange(harmonic_index_array, dtype=jnp.float32)
    degree_ints = jnp.arange(harmonic_index_array, dtype=jnp.int32)
    even_mask = (my_orders[:, None] + degree_ints[None, :]) % 2 == 0
    parity_sign = jnp.where(even_mask, 1.0, -1.0)
    above_diag = degree_vals[None, :] > order_float[:, None]
    link_coef = jnp.where(
        above_diag,
        jnp.sqrt(
            jnp.maximum(
                (2.0 * degree_vals + 1.0)
                * (degree_vals * degree_vals - order_float[:, None] * order_float[:, None]),
                0.0,
            )
            / jnp.maximum(2.0 * degree_vals - 1.0, 1.0)
        ),
        0.0,
    )
    theta_all = math.pi * (jnp.arange(NLAT, dtype=jnp.float32) + 0.5) / NLAT
    cosine_all = jnp.cos(theta_all)
    cosine_north = cosine_all[:north_count]
    sine_north = jnp.sin(theta_all[:north_count])
    weights = fejer_weights(north_count, NLAT)
    legendre_all = legendre_rows(order_float, cosine_north, sine_north, harmonic_index_array)
    coupled_quantities = jnp.stack([thermal_spectra, induction_potential])
    motion_groupings = jnp.stack([toroidal_stream_spectra, thermal_spectra, induction_potential])
    weighted = motion_groupings * degree_vals
    product = motion_groupings * link_coef[None, None, None]
    lifted = jnp.concatenate([product[..., 1:], jnp.zeros_like(product[..., :1])], axis=-1)
    coef_sets = jnp.concatenate(
        [motion_groupings, weighted, lifted, outward_speed_spectra[None]], axis=0
    )
    set_count = 10
    coeffs = jnp.transpose(coef_sets, (3, 0, 2, 1, 4)).reshape(
        local_azimuthal_numbers, set_count * layer_indices * 2, harmonic_index_array
    )
    column_count = coeffs.shape[1]
    stacked = jnp.concatenate([coeffs, coeffs * parity_sign[:, None, :]], axis=1)
    result = jnp.einsum("ocl,oln->ocn", stacked, legendre_all, precision=highest)
    result = jnp.concatenate(
        [result[:, :column_count], jnp.flip(result[:, column_count:], axis=2)], axis=2
    ).reshape(local_azimuthal_numbers, set_count, layer_indices, 2, NLAT)
    plain_part = result[:, 0:3]
    slant_part = cosine_all * result[:, 3:6] - result[:, 6:9]
    outgoing = jnp.concatenate([plain_part, slant_part, result[:, 9:10]], axis=1)
    arrived = lax.all_to_all(outgoing, "ma", split_axis=4, concat_axis=0, tiled=True)
    spin_all = position_azimuth_map.astype(jnp.float32)[:, None, None, None]
    base_part = arrived[:, 0:3]
    turned_all = jnp.stack(
        [-spin_all * base_part[:, :, :, 1], spin_all * base_part[:, :, :, 0]], axis=3
    )
    full_sets = jnp.concatenate([turned_all, arrived[:, 3:7], base_part[:, 1:3]], axis=1)
    grid_sets = to_longitudes(full_sets, position_azimuth_map, NLON)
    padded = extended(grid_sets[7:9], (("row", 1),), 1)
    depthwise_slope = (padded[:, 2:] - padded[:, :-2]) / (2.0 * spacing)
    grid_sets = jnp.concatenate([grid_sets[0:7], depthwise_slope], axis=0)
    lat_index = lax.axis_index("ma") * latitude_rows + jnp.arange(latitude_rows, dtype=jnp.int32)
    theta_mine = math.pi * (lat_index.astype(jnp.float32) + 0.5) / NLAT
    sine_mine = jnp.sin(theta_mine)
    shell_index = lax.axis_index("row") * layer_indices + jnp.arange(layer_indices, dtype=jnp.int32)
    radius = inner_radius + spacing * (shell_index.astype(jnp.float32) + 0.5)
    factor = 1.0 / (radius[:, None] * radius[:, None] * (sine_mine * sine_mine)[None, :])
    forcing = nonlinear(grid_sets, factor[:, :, None])
    spectra = from_longitudes(forcing, position_azimuth_map, NLON)
    returned = lax.all_to_all(spectra, "ma", split_axis=0, concat_axis=4, tiled=True)
    values = returned.reshape(local_azimuthal_numbers, 4 * layer_indices, NLAT)
    column_count = values.shape[1]
    north_part = values[:, :, :north_count]
    south_part = jnp.flip(values[:, :, north_count:], axis=2)
    stacked = jnp.concatenate(
        [(north_part + south_part) * weights, (north_part - south_part) * weights], axis=1
    )
    result = jnp.einsum("ocn,oln->ocl", stacked, legendre_all, precision=highest)
    tendency = jnp.where(even_mask[:, None, :], result[:, :column_count], result[:, column_count:])
    tendency = jnp.transpose(
        tendency.reshape(local_azimuthal_numbers, 2, layer_indices, 2, harmonic_index_array),
        (1, 3, 2, 0, 4),
    )
    right_side = coupled_quantities + time_step * tendency
    keep_low = 1.0 - subdiagonal_complement
    keep_up = 1.0 - superdiagonal_complement
    unit_gains = jnp.ones((2, harmonic_index_array), jnp.float32)
    zero_block = jnp.zeros(right_side[:, :, 0].shape, jnp.float32)
    running_sum = zero_block
    through = unit_gains
    each_shell = 0
    running_sum = (
        right_side[:, :, each_shell] + keep_low[:, each_shell][:, None, None, :] * running_sum
    )
    through = through * keep_low[:, each_shell]
    entering = entering_2(
        (through, running_sum), "row", join_maps, (unit_gains, zero_block), False
    )[1]
    running = entering
    each_shell = 0
    running = right_side[:, :, each_shell] + keep_low[:, each_shell][:, None, None, :] * running
    scaled = [running / diagonal_entries[:, each_shell][:, None, None, :]]
    running_sum = zero_block
    through = unit_gains
    for each_shell in reversed(range(layer_indices)):
        running_sum = scaled[each_shell] + keep_up[:, each_shell][:, None, None, :] * running_sum
        through = through * keep_up[:, each_shell]
    entering = entering_2((through, running_sum), "row", join_maps, (unit_gains, zero_block), True)[
        1
    ]
    running = entering
    results = []
    for each_shell in reversed(range(layer_indices)):
        running = scaled[each_shell] + keep_up[:, each_shell][:, None, None, :] * running
        results.append(running)
    solved = jnp.stack(results[::-1], axis=2)
    return (solved[0], solved[1])


VMEM_BYTES = 60 * 1024 * 1024
SET_ROWS = 48
PROFILE_ROWS = 32


def halves(values):
    high = values.astype(jnp.bfloat16)
    return high, (values - high.astype(jnp.float32)).astype(jnp.bfloat16)


def dot(left, right):
    return jnp.dot(left, right, preferred_element_type=jnp.float32)


def dot_t(left, right):
    return lax.dot_general(
        left, right, (((1,), (1,)), ((), ())), preferred_element_type=jnp.float32
    )


def synthesis_kernel(
    psi_ref, heat_ref, mag_ref, speed_ref, link_ref, sign_ref, rise_ref, fall_ref, diag_ref,
    log_ref, cos_ref, out_ref, high_ref, low_ref, table, coef, prof, *, step_count,
):
    step = pl.program_id(0)
    group, degrees = link_ref.shape
    north = cos_ref.shape[1]
    local = group * step_count
    targets, quantities, rows, lanes = out_ref.shape
    half = rows // 2

    @pl.when(step == 0)
    def _():
        coef[...] = jnp.zeros_like(coef)

    degree = lax.broadcasted_iota(jnp.int32, (group, degrees), 1).astype(jnp.float32)
    link = link_ref[...]
    sign = sign_ref[...]
    for q, ref in enumerate((psi_ref, heat_ref, mag_ref, speed_ref)):
        for c in range(2):
            plain = ref[c, 0]
            sets = [(2 * q + c, plain)]
            if q < 3:
                sets.append((8 + 2 * q + c, plain * degree))
                sets.append((16 + 2 * q + c, pltpu.roll(plain * link, degrees - 1, 1)))
            for row, value in sets:
                signed = value * sign
                for a in range(degrees // 128):
                    cut = slice(a * 128, (a + 1) * 128)
                    coef[a, pl.ds(row, group, stride=SET_ROWS), :] = value[:, cut]
                    coef[a, pl.ds(SET_ROWS // 2 + row, group, stride=SET_ROWS), :] = signed[:, cut]

    cosine = jnp.broadcast_to(cos_ref[...], (group, north))
    zero = jnp.zeros((group, north), jnp.float32)

    def sweep(position, state):
        before, current, log_scale = state
        base = pl.multiple_of(position * 128, 128)
        rise = rise_ref[:, pl.ds(base, 128)]
        fall = fall_ref[:, pl.ds(base, 128)]
        diag = diag_ref[:, pl.ds(base, 128)]
        for part in range(4):
            scale = jnp.exp(log_scale)
            for offset in range(32):
                i = part * 32 + offset
                fresh = (
                    rise[:, i : i + 1] * cosine * current
                    - fall[:, i : i + 1] * before
                    + diag[:, i : i + 1]
                )
                before, current = current, fresh
                row = fresh * scale
                start = pl.multiple_of((base + i) * group, group)
                for a in range(north // 128):
                    table[a, pl.ds(start, group), :] = row[:, a * 128 : (a + 1) * 128]
            magnitude = jnp.maximum(jnp.abs(before), jnp.abs(current))
            magnitude = jnp.where(magnitude > 0.0, magnitude, 1.0)
            before = before / magnitude
            current = current / magnitude
            log_scale = log_scale + jnp.log(magnitude)
        return before, current, log_scale

    lax.fori_loop(0, degrees // 128, sweep, (zero, zero, log_ref[...]))

    def one_order(m, carry):
        values = jnp.concatenate(
            [table[a, pl.ds(m, degrees, stride=group), :] for a in range(north // 128)], axis=1
        )
        high, low = halves(values)
        high_ref[m] = high
        low_ref[m] = low
        start = pl.multiple_of(m * SET_ROWS, SET_ROWS)
        rows = jnp.concatenate(
            [coef[a, pl.ds(start, SET_ROWS), :] for a in range(degrees // 128)], axis=1
        )
        rows_high, rows_low = halves(rows)
        both = dot(jnp.concatenate([rows_high, rows_low], axis=0), high)
        result = both[:SET_ROWS] + both[SET_ROWS:] + dot(rows_high, low)
        wide = jnp.broadcast_to(cos_ref[...], (8, north))
        pieces = jnp.concatenate(
            [
                result[0:8],
                wide * result[8:16] - result[16:24],
                result[24:32],
                -wide * result[32:40] - result[40:48],
            ],
            axis=0,
        )
        first = pl.multiple_of((step * group + m) * PROFILE_ROWS, PROFILE_ROWS)
        for a in range(north // 128):
            prof[a, pl.ds(first, PROFILE_ROWS), :] = pieces[:, a * 128 : (a + 1) * 128]
        return carry

    lax.fori_loop(0, group, one_order, 0)

    @pl.when(step == step_count - 1)
    def _():
        places = [0, 2, 4, 8, 10, 12, 6]
        for side in range(2):
            for q, place in enumerate(places):
                first = side * 16 + place
                for a in range(north // 128):
                    block = jnp.concatenate(
                        [
                            prof[a, pl.ds(first + c, local, stride=PROFILE_ROWS), :]
                            for c in range(2)
                        ],
                        axis=0,
                    )
                    turned = block.T
                    lat = a * 128
                    while lat < (a + 1) * 128:
                        target, offset = divmod(lat, half)
                        count = min(half - offset, (a + 1) * 128 - lat)
                        out_ref[target, q, pl.ds(side * half + offset, count), :] = turned[
                            lat - a * 128 : lat - a * 128 + count
                        ]
                        lat += count


def synthesis(spectra, link, sign, rise, fall, diag, log_start, cosine, step_count, targets):
    local, degrees = link.shape
    north = cosine.shape[1]
    group = local // step_count
    spec = pl.BlockSpec((2, 1, group, degrees), lambda g: (0, 0, g, 0))
    table_spec = pl.BlockSpec((group, degrees), lambda g: (g, 0))
    legendre_spec = pl.BlockSpec((group, degrees, north), lambda g: (g, 0, 0))
    out_shape = (targets, 7, 2 * (north // targets), 2 * local)
    return pl.pallas_call(
        functools.partial(synthesis_kernel, step_count=step_count),
        grid=(step_count,),
        in_specs=[spec] * 4
        + [table_spec] * 5
        + [
            pl.BlockSpec((group, north), lambda g: (g, 0)),
            pl.BlockSpec((1, north), lambda g: (0, 0)),
        ],
        out_specs=[
            pl.BlockSpec(out_shape, lambda g: (0, 0, 0, 0)),
            legendre_spec,
            legendre_spec,
        ],
        out_shape=[
            jax.ShapeDtypeStruct(out_shape, jnp.float32),
            jax.ShapeDtypeStruct((local, degrees, north), jnp.bfloat16),
            jax.ShapeDtypeStruct((local, degrees, north), jnp.bfloat16),
        ],
        scratch_shapes=[
            pltpu.VMEM((north // 128, group * degrees, 128), jnp.float32),
            pltpu.VMEM((degrees // 128, group * SET_ROWS, 128), jnp.float32),
            pltpu.VMEM((north // 128, local * PROFILE_ROWS, 128), jnp.float32),
        ],
        compiler_params=pltpu.CompilerParams(vmem_limit_bytes=VMEM_BYTES),
        cost_estimate=pl.CostEstimate(
            flops=2 * 3 * SET_ROWS * local * degrees * north,
            bytes_accessed=4 * local * degrees * north,
            transcendentals=0,
        ),
        name="synthesis",
    )(*spectra, link, sign, rise, fall, diag, log_start, cosine)


def grid_kernel(
    here_ref, above_ref, below_ref, weight_ref, spin_ref, high_ref, low_ref, factor_ref,
    out_ref, sets, total, *, step_count, slope_scale, lon_total,
):
    step = pl.program_id(0)
    sources, _, rows, lanes = here_ref.shape
    count = 9 * rows

    @pl.when(step == 0)
    def _():
        total[...] = jnp.zeros_like(total)
        for source in range(sources):
            cut = slice(source * lanes, (source + 1) * lanes)
            weight = weight_ref[:, cut]
            spin = spin_ref[:, cut]
            for q in range(9):
                if q < 3:
                    value = pltpu.roll(here_ref[source, q], lanes // 2, 1) * spin
                elif q < 7:
                    value = here_ref[source, q] * weight
                else:
                    value = (above_ref[source, q - 7] - below_ref[source, q - 7]) * (
                        weight * slope_scale
                    )
                high, low = halves(value)
                sets[q * rows : (q + 1) * rows, cut] = high
                sets[count + q * rows : count + (q + 1) * rows, cut] = low

    both = dot(sets[...], high_ref[...])
    grids = both[:count] + both[count:] + dot(sets[:count], low_ref[...])
    g = [grids[q * rows : (q + 1) * rows] for q in range(9)]
    factor = factor_ref[...]
    heat = -((g[3] * g[1] - g[0] * g[4]) * factor + g[6] * g[7])
    induction = -((g[3] * g[2] - g[0] * g[5]) * factor + g[6] * g[8])
    high, low = halves(jnp.concatenate([heat, induction], axis=0))
    back = dot_t(jnp.concatenate([high, low], axis=0), high_ref[...])
    total[...] += back[: 2 * rows] + back[2 * rows :] + dot_t(high, low_ref[...])

    @pl.when(step == step_count - 1)
    def _():
        for source in range(sources):
            cut = slice(source * lanes, (source + 1) * lanes)
            for f in range(2):
                out_ref[source, f] = total[f * rows : (f + 1) * rows, cut] * (1.0 / lon_total)


def grid_step(here, above, below, weight, spin, wave_high, wave_low, factor, slope_scale):
    sources, _, rows, lanes = here.shape
    waves, lon_total = wave_high.shape
    lon_block = math.gcd(256, lon_total)
    step_count = lon_total // lon_block
    whole = lambda shape: pl.BlockSpec(shape, lambda i: (0,) * len(shape))
    wave_spec = pl.BlockSpec((waves, lon_block), lambda i: (0, i))
    out_shape = (sources, 2, rows, lanes)
    return pl.pallas_call(
        functools.partial(
            grid_kernel, step_count=step_count, slope_scale=slope_scale, lon_total=lon_total
        ),
        grid=(step_count,),
        in_specs=[
            whole(here.shape), whole(above.shape), whole(below.shape),
            whole(weight.shape), whole(spin.shape), wave_spec, wave_spec, whole(factor.shape),
        ],
        out_specs=whole(out_shape),
        out_shape=jax.ShapeDtypeStruct(out_shape, jnp.float32),
        scratch_shapes=[
            pltpu.VMEM((18 * rows, waves), jnp.bfloat16),
            pltpu.VMEM((2 * rows, waves), jnp.float32),
        ],
        compiler_params=pltpu.CompilerParams(vmem_limit_bytes=VMEM_BYTES),
        cost_estimate=pl.CostEstimate(
            flops=2 * 3 * 11 * rows * waves * lon_total,
            bytes_accessed=4 * waves * lon_total,
            transcendentals=0,
        ),
        name="grid_step",
    )(here, above, below, weight, spin, wave_high, wave_low, factor)


def analysis_kernel(
    back_ref, quad_ref, sign_ref, heat_ref, mag_ref, high_ref, low_ref, out_ref,
    values, tend, *, step_count,
):
    step = pl.program_id(0)
    blocks, _, rows, lanes = back_ref.shape
    half = rows // 2
    local = lanes // 2
    group = local // step_count
    north = quad_ref.shape[1]

    @pl.when(step == 0)
    def _():
        for f in range(2):
            sides = []
            for side in range(2):
                stacked = jnp.concatenate(
                    [back_ref[b, f, side * half : (side + 1) * half] for b in range(blocks)], axis=0
                )
                sides.append(stacked.T)
            quad = quad_ref[...]
            for sign, mixed in enumerate((sides[0] + sides[1], sides[0] - sides[1])):
                mixed = mixed * quad
                for c in range(2):
                    row = sign * 4 + f * 2 + c
                    for a in range(north // 128):
                        values[a, pl.ds(row, local, stride=8), :] = mixed[
                            c * local : (c + 1) * local, a * 128 : (a + 1) * 128
                        ]

    def one_order(m, carry):
        start = pl.multiple_of((step * group + m) * 8, 8)
        rows_in = jnp.concatenate(
            [values[a, pl.ds(start, 8), :] for a in range(north // 128)], axis=1
        )
        row_high = rows_in.astype(jnp.bfloat16).astype(jnp.float32)
        row_low = rows_in - row_high
        both = jnp.concatenate([row_high, row_low], axis=0).astype(jnp.bfloat16)
        first = dot_t(both, high_ref[m])
        second = dot_t(both, low_ref[m])
        result = first[:8] + first[8:] + second[:8]
        for a in range(result.shape[1] // 128):
            tend[a, pl.ds(pl.multiple_of(m * 8, 8), 8), :] = result[:, a * 128 : (a + 1) * 128]
        return carry

    lax.fori_loop(0, group, one_order, 0)
    even = sign_ref[...] > 0.0
    for f, ref in enumerate((heat_ref, mag_ref)):
        for c in range(2):
            parts = [
                jnp.concatenate(
                    [
                        tend[a, pl.ds(sign * 4 + f * 2 + c, group, stride=8), :]
                        for a in range(even.shape[1] // 128)
                    ],
                    axis=1,
                )
                for sign in range(2)
            ]
            out_ref[0, f, c] = ref[c, 0] + time_step * jnp.where(even, parts[0], parts[1])


def analysis(back, quad, sign, heat, mag, high, low, step_count):
    local, degrees, north = high.shape
    group = local // step_count
    spec = pl.BlockSpec((2, 1, group, degrees), lambda g: (0, 0, g, 0))
    legendre_spec = pl.BlockSpec((group, degrees, north), lambda g: (g, 0, 0))
    return pl.pallas_call(
        functools.partial(analysis_kernel, step_count=step_count),
        grid=(step_count,),
        in_specs=[
            pl.BlockSpec(back.shape, lambda g: (0, 0, 0, 0)),
            pl.BlockSpec(quad.shape, lambda g: (0, 0)),
            pl.BlockSpec((group, degrees), lambda g: (g, 0)),
            spec, spec, legendre_spec, legendre_spec,
        ],
        out_specs=pl.BlockSpec((1, 2, 2, group, degrees), lambda g: (g, 0, 0, 0, 0)),
        out_shape=jax.ShapeDtypeStruct((step_count, 2, 2, group, degrees), jnp.float32),
        scratch_shapes=[
            pltpu.VMEM((north // 128, local * 8, 128), jnp.float32),
            pltpu.VMEM((degrees // 128, group * 8, 128), jnp.float32),
        ],
        compiler_params=pltpu.CompilerParams(vmem_limit_bytes=VMEM_BYTES),
        cost_estimate=pl.CostEstimate(
            flops=2 * 3 * 8 * local * degrees * north,
            bytes_accessed=4 * local * degrees * north,
            transcendentals=0,
        ),
        name="analysis",
    )(back, quad, sign, heat, mag, high, low)


def wave_halves(orders, lon_total):
    width = 128
    def pair(columns):
        phase_int = orders[:, None] * columns[None, :] % lon_total
        angle_vals = 2.0 * math.pi / lon_total * phase_int.astype(jnp.float32)
        return jnp.cos(angle_vals), jnp.sin(angle_vals)

    fine_cos, fine_sin = pair(jnp.arange(width, dtype=jnp.int32))
    far_cos, far_sin = pair(jnp.arange(lon_total // width, dtype=jnp.int32) * width)
    cos_parts, sin_parts = [], []
    for a in range(lon_total // width):
        ca, sa = far_cos[:, a : a + 1], far_sin[:, a : a + 1]
        cos_parts.append(ca * fine_cos - sa * fine_sin)
        sin_parts.append(-(sa * fine_cos + ca * fine_sin))
    return jnp.concatenate(cos_parts, axis=1), jnp.concatenate(sin_parts, axis=1)


def kernel_body(
    toroidal_stream_spectra,
    thermal_spectra,
    induction_potential,
    outward_speed_spectra,
    position_azimuth_map,
    subdiagonal_complement,
    superdiagonal_complement,
    diagonal_entries,
):
    row_count = lax.axis_size("row")
    ma_count = lax.axis_size("ma")
    local = thermal_spectra.shape[2]
    degrees = thermal_spectra.shape[3]
    north = NLAT // 2
    half = north // ma_count
    spacing = shell_span / row_count

    small = jnp.stack([subdiagonal_complement, superdiagonal_complement, diagonal_entries])
    row_index = lax.axis_index("row")
    factors = jnp.zeros((row_count,) + small.shape, jnp.float32)
    factors = lax.dynamic_update_slice_in_dim(factors, small[None], row_index, 0)
    for shift in range(1, row_count):
        moved = lax.ppermute(
            small, "row", [(i, (i + shift) % row_count) for i in range(row_count)]
        )
        factors = lax.dynamic_update_slice_in_dim(
            factors, moved[None], (row_index + row_count - shift) % row_count, 0
        )
    factors = factors[:, :, :, 0]

    slot_start = lax.axis_index("ma") * local
    my_orders = lax.dynamic_slice_in_dim(position_azimuth_map, slot_start, local)
    order_col = my_orders.astype(jnp.float32)[:, None]
    degree = jnp.arange(degrees, dtype=jnp.float32)[None, :]
    degree_ints = jnp.arange(degrees, dtype=jnp.int32)
    even_mask = (my_orders[:, None] + degree_ints[None, :]) % 2 == 0
    sign = jnp.where(even_mask, 1.0, -1.0)
    above_diag = degree > order_col
    square = degree * degree - order_col * order_col
    link = jnp.where(
        above_diag,
        jnp.sqrt(
            jnp.maximum((2.0 * degree + 1.0) * square, 0.0) / jnp.maximum(2.0 * degree - 1.0, 1.0)
        ),
        0.0,
    )
    denominator = jnp.where(above_diag, square, 1.0)
    rise = jnp.where(
        above_diag, jnp.sqrt(jnp.maximum(4.0 * degree * degree - 1.0, 1.0) / denominator), 0.0
    )
    lower_term = (degree - 1.0) * (degree - 1.0) - order_col * order_col
    fall = jnp.where(
        above_diag,
        jnp.sqrt(
            jnp.maximum((2.0 * degree + 1.0) * lower_term, 0.0)
            / (jnp.maximum(2.0 * degree - 3.0, 1.0) * denominator)
        ),
        0.0,
    )
    diag = jnp.where(degree == order_col, 1.0, 0.0)
    theta = math.pi * (jnp.arange(NLAT, dtype=jnp.float32) + 0.5) / NLAT
    cosine = jnp.cos(theta)[None, :north]
    sine = jnp.sin(theta)[None, :north]
    log_start = (
        0.5 * (lax.lgamma(order_col + 1.5) - lax.lgamma(order_col + 1.0) - log_gamma_half)
        - 0.5 * math.log(2.0)
        + order_col * jnp.log(sine)
    )
    outgoing, high, low = synthesis(
        (toroidal_stream_spectra, thermal_spectra, induction_potential, outward_speed_spectra),
        link, sign, rise, fall, diag, log_start, cosine, row_count, ma_count,
    )
    here = lax.all_to_all(outgoing, "ma", 0, 0, tiled=True)

    cos_wave, sin_wave = wave_halves(position_azimuth_map, NLON)
    wave = jnp.stack(
        [cos_wave.reshape(ma_count, local, NLON), sin_wave.reshape(ma_count, local, NLON)], axis=1
    ).reshape(2 * ma_count * local, NLON)
    rounded = lax.reduce_precision(wave, 8, 7)
    wave_high = rounded.astype(jnp.bfloat16)
    wave_low = (wave - rounded).astype(jnp.bfloat16)
    orders = position_azimuth_map.astype(jnp.float32).reshape(ma_count, 1, local)
    weight = jnp.where(orders == 0.0, 1.0, 2.0)
    spin = jnp.concatenate([-orders * weight, orders * weight], axis=1).reshape(1, -1)
    weight = jnp.concatenate([weight, weight], axis=1).reshape(1, -1)

    forward = [(i, i + 1) for i in range(row_count - 1)]
    backward = [(target, source) for source, target in forward]
    profiles = here[:, 1:3]
    below = lax.ppermute(profiles, "row", forward)
    above = lax.ppermute(profiles, "row", backward)

    lat_index = lax.axis_index("ma") * half + jnp.arange(half, dtype=jnp.int32)
    sine_mine = jnp.sin(math.pi * (lat_index.astype(jnp.float32) + 0.5) / NLAT)
    radius = inner_radius + spacing * (row_index.astype(jnp.float32) + 0.5)
    factor = 1.0 / (radius * radius * (sine_mine * sine_mine))
    factor = jnp.concatenate([factor, factor])[:, None]
    spectra = grid_step(
        here, above, below, weight, spin, wave_high, wave_low, factor, 1.0 / (2.0 * spacing)
    )
    back = lax.all_to_all(spectra, "ma", 0, 0, tiled=True)

    quad = fejer_weights(north, NLAT)[None, :]
    right_side = analysis(
        back, quad, sign, thermal_spectra, induction_potential, high, low, row_count
    )
    shells = lax.all_to_all(right_side, "row", 0, 0, tiled=True)
    spread = lambda k, which: factors[k, which][:, None, None, :]
    running = jnp.zeros_like(shells[0])
    scaled = []
    for k in range(row_count):
        running = shells[k] + (1.0 - spread(k, 0)) * running
        scaled.append(running / spread(k, 2))
    running = jnp.zeros_like(shells[0])
    solved = []
    for k in reversed(range(row_count)):
        running = scaled[k] + (1.0 - spread(k, 1)) * running
        solved.append(running)
    solved = lax.all_to_all(jnp.stack(solved[::-1]), "row", 0, 0, tiled=True)
    solved = jnp.transpose(solved, (1, 2, 0, 3, 4)).reshape(2, 2, 1, local, degrees)
    return solved[0], solved[1]


def program(*args):
    row_count = lax.axis_size("row")
    ma_count = lax.axis_size("ma")
    _, shells, local, degrees = args[1].shape
    fits = (
        shells == 1
        and (NLAT // 2) % (8 * ma_count) == 0
        and (2 * local) % 128 == 0
        and local % (16 * row_count) == 0
        and degrees % 128 == 0
        and (NLAT // 2) % 128 == 0
        and NLON % 128 == 0
    )
    return kernel_body(*args) if fits else body(*args)


def solution(mesh):
    in_specs = (
        P(None, "row", "ma", None),
        P(None, "row", "ma", None),
        P(None, "row", "ma", None),
        P(None, "row", "ma", None),
        P(),
        P(None, "row", None),
        P(None, "row", None),
        P(None, "row", None),
    )
    out_specs = (P(None, "row", "ma", None), P(None, "row", "ma", None))
    return jax.shard_map(program, mesh=mesh, in_specs=in_specs, out_specs=out_specs, check_vma=False)
```

```python
import functools
import math

import jax
import jax.numpy as jnp
from jax import lax
from jax.experimental import pallas as pl
from jax.experimental.pallas import tpu as pltpu
from jax.sharding import PartitionSpec as P

NLAT = 768
NLON = 1536


inner_radius = 0.35
shell_span = 0.65
time_step = 0.001
highest = lax.Precision.HIGHEST
log_gamma_half = 0.5 * math.log(math.pi) - math.log(2.0)


def extended(block, sides, width):
    for axis, dim in sides:
        count = lax.axis_size(axis)
        forward = [(i, i + 1) for i in range(count - 1)]
        backward = [(target, source) for source, target in forward]
        low = lax.ppermute(
            lax.slice_in_dim(block, block.shape[dim] - width, None, axis=dim), axis, forward
        )
        high = lax.ppermute(lax.slice_in_dim(block, 0, width, axis=dim), axis, backward)
        block = jnp.concatenate([low, block, high], axis=dim)
    return block


def entering_2(part, axis, combine, identity, reverse):
    count = lax.axis_size(axis)
    place = lax.axis_index(axis)
    ahead = count - 1 - place if reverse else place
    gathered = jax.tree.map(lambda a: lax.all_gather(a, axis), part)
    state = jax.tree.map(lambda a, e: jnp.zeros_like(a) + jnp.asarray(e, a.dtype), part, identity)

    def one(step, state):
        source = count - 1 - step if reverse else step
        return combine(
            state, jax.tree.map(lambda a: lax.dynamic_index_in_dim(a, source, 0, False), gathered)
        )

    return lax.fori_loop(0, ahead, one, state)


def legendre_rows(orders, cosine, sine_vals, harmonic_index_array):
    block_len = math.gcd(32, harmonic_index_array)
    dtype_ref = cosine.dtype
    order_col = orders[:, None]
    log_start = (
        0.5 * (lax.lgamma(order_col + 1.5) - lax.lgamma(order_col + 1.0) - log_gamma_half)
        - 0.5 * math.log(2.0)
        + order_col * jnp.log(sine_vals)[None, :]
    )
    zero_state = jnp.zeros(log_start.shape, dtype_ref)
    legendre = jnp.zeros((orders.shape[0], harmonic_index_array, cosine.shape[0]), dtype_ref)

    def sweep(position, state_tuple):
        before, current, log_scale, legendre = state_tuple
        new_rows = []
        for offset in range(block_len):
            degree_now = (position * block_len + offset).astype(dtype_ref)
            above_diag = degree_now > order_col
            square = degree_now * degree_now - order_col * order_col
            denominator = jnp.where(above_diag, square, 1.0)
            rise_coef = jnp.where(
                above_diag,
                jnp.sqrt(jnp.maximum(4.0 * degree_now * degree_now - 1.0, 1.0) / denominator),
                0.0,
            )
            lower_term = (degree_now - 1.0) * (degree_now - 1.0) - order_col * order_col
            fall_coef = jnp.where(
                above_diag,
                jnp.sqrt(
                    jnp.maximum((2.0 * degree_now + 1.0) * lower_term, 0.0)
                    / (jnp.maximum(2.0 * degree_now - 3.0, 1.0) * denominator)
                ),
                0.0,
            )
            fresh_row = jnp.where(
                degree_now == order_col,
                1.0,
                rise_coef * cosine[None, :] * current - fall_coef * before,
            )
            before, current = (current, fresh_row)
            new_rows.append(fresh_row * jnp.exp(log_scale))
        magnitude = jnp.maximum(jnp.abs(before), jnp.abs(current))
        magnitude = jnp.where(magnitude > 0.0, magnitude, 1.0)
        before = before / magnitude
        current = current / magnitude
        log_scale = log_scale + jnp.log(magnitude)
        first_row = (position * block_len).astype(jnp.int32)
        legendre = lax.dynamic_update_slice(
            legendre, jnp.stack(new_rows, axis=1), (jnp.int32(0), first_row, jnp.int32(0))
        )
        return (before, current, log_scale, legendre)

    state_tuple = lax.fori_loop(
        0, harmonic_index_array // block_len, sweep, (zero_state, zero_state, log_start, legendre)
    )
    return state_tuple[3]


def wave_table(orders, first_col, column_count, lon_total):
    column_ids = first_col + jnp.arange(column_count, dtype=jnp.int32)
    phase_int = orders[:, None] * column_ids[None, :] % lon_total
    angle_vals = 2.0 * math.pi / lon_total * phase_int.astype(jnp.float32)
    return jnp.stack([jnp.cos(angle_vals), -jnp.sin(angle_vals)], axis=1)


def to_longitudes(spectra, orders, lon_total):
    order_weight = jnp.where(orders == 0, 1.0, 2.0).astype(spectra.dtype)
    weighted = spectra * order_weight[:, None, None, None, None]
    lon_block = math.gcd(512, lon_total)
    output_buf = jnp.zeros(
        (spectra.shape[1], spectra.shape[2], spectra.shape[4], lon_total), spectra.dtype
    )

    def place(position, output_buf):
        first_col = (position * lon_block).astype(jnp.int32)
        wave_block = wave_table(orders, first_col, lon_block, lon_total)
        grid_piece = jnp.einsum("mfscn,mcp->fsnp", weighted, wave_block, precision=highest)
        return lax.dynamic_update_slice(
            output_buf, grid_piece, (jnp.int32(0), jnp.int32(0), jnp.int32(0), first_col)
        )

    return lax.fori_loop(0, lon_total // lon_block, place, output_buf)


def from_longitudes(grid_sets, orders, lon_total):
    lon_block = math.gcd(512, lon_total)
    running_sum = jnp.zeros(
        (orders.shape[0], grid_sets.shape[0], grid_sets.shape[1], 2, grid_sets.shape[2]),
        grid_sets.dtype,
    )

    def add_block(position, running_sum):
        first_col = (position * lon_block).astype(jnp.int32)
        wave_block = wave_table(orders, first_col, lon_block, lon_total)
        grid_piece = lax.dynamic_slice_in_dim(grid_sets, first_col, lon_block, 3)
        return running_sum + jnp.einsum(
            "fsnp,mcp->mfscn", grid_piece, wave_block, precision=highest
        )

    return lax.fori_loop(0, lon_total // lon_block, add_block, running_sum) / lon_total


def fejer_weights(node_count, lat_total):
    term_count = lat_total // 2
    wave_ints = jnp.arange(1, term_count + 1, dtype=jnp.int32)
    node_ints = 2 * jnp.arange(node_count, dtype=jnp.int32) + 1
    phase_int = wave_ints[:, None] * node_ints[None, :] % (2 * lat_total)
    cosines = jnp.cos(math.pi / lat_total * phase_int.astype(jnp.float32))
    wave_vals = wave_ints.astype(jnp.float32)
    ratio_vals = cosines / (4.0 * wave_vals * wave_vals - 1.0)[:, None]
    return 2.0 / lat_total * (1.0 - 2.0 * jnp.sum(ratio_vals, axis=0))


def nonlinear(grid_sets, factor):
    heat_term = -(
        (grid_sets[3] * grid_sets[1] - grid_sets[0] * grid_sets[4]) * factor
        + grid_sets[6] * grid_sets[7]
    )
    field_term = -(
        (grid_sets[3] * grid_sets[2] - grid_sets[0] * grid_sets[5]) * factor
        + grid_sets[6] * grid_sets[8]
    )
    return jnp.stack([heat_term, field_term])


def join_maps(earlier_map, later_map):
    return (
        earlier_map[0] * later_map[0],
        earlier_map[1] * later_map[0][:, None, None, :] + later_map[1],
    )


def body(
    toroidal_stream_spectra,
    thermal_spectra,
    induction_potential,
    outward_speed_spectra,
    position_azimuth_map,
    subdiagonal_complement,
    superdiagonal_complement,
    diagonal_entries,
):
    layer_indices = thermal_spectra.shape[1]
    local_azimuthal_numbers = thermal_spectra.shape[2]
    harmonic_index_array = thermal_spectra.shape[3]
    latitude_rows = NLAT // lax.axis_size("ma")
    north_count = NLAT // 2
    spacing = shell_span / (layer_indices * lax.axis_size("row"))
    slot_start = lax.axis_index("ma") * local_azimuthal_numbers
    my_orders = lax.dynamic_slice_in_dim(position_azimuth_map, slot_start, local_azimuthal_numbers)
    order_float = my_orders.astype(jnp.float32)
    degree_vals = jnp.arange(harmonic_index_array, dtype=jnp.float32)
    degree_ints = jnp.arange(harmonic_index_array, dtype=jnp.int32)
    even_mask = (my_orders[:, None] + degree_ints[None, :]) % 2 == 0
    parity_sign = jnp.where(even_mask, 1.0, -1.0)
    above_diag = degree_vals[None, :] > order_float[:, None]
    link_coef = jnp.where(
        above_diag,
        jnp.sqrt(
            jnp.maximum(
                (2.0 * degree_vals + 1.0)
                * (degree_vals * degree_vals - order_float[:, None] * order_float[:, None]),
                0.0,
            )
            / jnp.maximum(2.0 * degree_vals - 1.0, 1.0)
        ),
        0.0,
    )
    theta_all = math.pi * (jnp.arange(NLAT, dtype=jnp.float32) + 0.5) / NLAT
    cosine_all = jnp.cos(theta_all)
    cosine_north = cosine_all[:north_count]
    sine_north = jnp.sin(theta_all[:north_count])
    weights = fejer_weights(north_count, NLAT)
    legendre_all = legendre_rows(order_float, cosine_north, sine_north, harmonic_index_array)
    coupled_quantities = jnp.stack([thermal_spectra, induction_potential])
    motion_groupings = jnp.stack([toroidal_stream_spectra, thermal_spectra, induction_potential])
    weighted = motion_groupings * degree_vals
    product = motion_groupings * link_coef[None, None, None]
    lifted = jnp.concatenate([product[..., 1:], jnp.zeros_like(product[..., :1])], axis=-1)
    coef_sets = jnp.concatenate(
        [motion_groupings, weighted, lifted, outward_speed_spectra[None]], axis=0
    )
    set_count = 10
    coeffs = jnp.transpose(coef_sets, (3, 0, 2, 1, 4)).reshape(
        local_azimuthal_numbers, set_count * layer_indices * 2, harmonic_index_array
    )
    column_count = coeffs.shape[1]
    stacked = jnp.concatenate([coeffs, coeffs * parity_sign[:, None, :]], axis=1)
    result = jnp.einsum("ocl,oln->ocn", stacked, legendre_all, precision=highest)
    result = jnp.concatenate(
        [result[:, :column_count], jnp.flip(result[:, column_count:], axis=2)], axis=2
    ).reshape(local_azimuthal_numbers, set_count, layer_indices, 2, NLAT)
    plain_part = result[:, 0:3]
    slant_part = cosine_all * result[:, 3:6] - result[:, 6:9]
    outgoing = jnp.concatenate([plain_part, slant_part, result[:, 9:10]], axis=1)
    arrived = lax.all_to_all(outgoing, "ma", split_axis=4, concat_axis=0, tiled=True)
    spin_all = position_azimuth_map.astype(jnp.float32)[:, None, None, None]
    base_part = arrived[:, 0:3]
    turned_all = jnp.stack(
        [-spin_all * base_part[:, :, :, 1], spin_all * base_part[:, :, :, 0]], axis=3
    )
    full_sets = jnp.concatenate([turned_all, arrived[:, 3:7], base_part[:, 1:3]], axis=1)
    grid_sets = to_longitudes(full_sets, position_azimuth_map, NLON)
    padded = extended(grid_sets[7:9], (("row", 1),), 1)
    depthwise_slope = (padded[:, 2:] - padded[:, :-2]) / (2.0 * spacing)
    grid_sets = jnp.concatenate([grid_sets[0:7], depthwise_slope], axis=0)
    lat_index = lax.axis_index("ma") * latitude_rows + jnp.arange(latitude_rows, dtype=jnp.int32)
    theta_mine = math.pi * (lat_index.astype(jnp.float32) + 0.5) / NLAT
    sine_mine = jnp.sin(theta_mine)
    shell_index = lax.axis_index("row") * layer_indices + jnp.arange(layer_indices, dtype=jnp.int32)
    radius = inner_radius + spacing * (shell_index.astype(jnp.float32) + 0.5)
    factor = 1.0 / (radius[:, None] * radius[:, None] * (sine_mine * sine_mine)[None, :])
    forcing = nonlinear(grid_sets, factor[:, :, None])
    spectra = from_longitudes(forcing, position_azimuth_map, NLON)
    returned = lax.all_to_all(spectra, "ma", split_axis=0, concat_axis=4, tiled=True)
    values = returned.reshape(local_azimuthal_numbers, 4 * layer_indices, NLAT)
    column_count = values.shape[1]
    north_part = values[:, :, :north_count]
    south_part = jnp.flip(values[:, :, north_count:], axis=2)
    stacked = jnp.concatenate(
        [(north_part + south_part) * weights, (north_part - south_part) * weights], axis=1
    )
    result = jnp.einsum("ocn,oln->ocl", stacked, legendre_all, precision=highest)
    tendency = jnp.where(even_mask[:, None, :], result[:, :column_count], result[:, column_count:])
    tendency = jnp.transpose(
        tendency.reshape(local_azimuthal_numbers, 2, layer_indices, 2, harmonic_index_array),
        (1, 3, 2, 0, 4),
    )
    right_side = coupled_quantities + time_step * tendency
    keep_low = 1.0 - subdiagonal_complement
    keep_up = 1.0 - superdiagonal_complement
    unit_gains = jnp.ones((2, harmonic_index_array), jnp.float32)
    zero_block = jnp.zeros(right_side[:, :, 0].shape, jnp.float32)
    running_sum = zero_block
    through = unit_gains
    each_shell = 0
    running_sum = (
        right_side[:, :, each_shell] + keep_low[:, each_shell][:, None, None, :] * running_sum
    )
    through = through * keep_low[:, each_shell]
    entering = entering_2(
        (through, running_sum), "row", join_maps, (unit_gains, zero_block), False
    )[1]
    running = entering
    each_shell = 0
    running = right_side[:, :, each_shell] + keep_low[:, each_shell][:, None, None, :] * running
    scaled = [running / diagonal_entries[:, each_shell][:, None, None, :]]
    running_sum = zero_block
    through = unit_gains
    for each_shell in reversed(range(layer_indices)):
        running_sum = scaled[each_shell] + keep_up[:, each_shell][:, None, None, :] * running_sum
        through = through * keep_up[:, each_shell]
    entering = entering_2((through, running_sum), "row", join_maps, (unit_gains, zero_block), True)[
        1
    ]
    running = entering
    results = []
    for each_shell in reversed(range(layer_indices)):
        running = scaled[each_shell] + keep_up[:, each_shell][:, None, None, :] * running
        results.append(running)
    solved = jnp.stack(results[::-1], axis=2)
    return (solved[0], solved[1])


VMEM_BYTES = 60 * 1024 * 1024
SET_ROWS = 48
PROFILE_ROWS = 32


def halves(values):
    high = values.astype(jnp.bfloat16)
    return high, (values - high.astype(jnp.float32)).astype(jnp.bfloat16)


def dot(left, right):
    return jnp.dot(left, right, preferred_element_type=jnp.float32)


def dot_t(left, right):
    return lax.dot_general(
        left, right, (((1,), (1,)), ((), ())), preferred_element_type=jnp.float32
    )


def synthesis_kernel(
    psi_ref, heat_ref, mag_ref, speed_ref, link_ref, sign_ref, rise_ref, fall_ref, diag_ref,
    log_ref, cos_ref, pair_ref, rest_ref, high_ref, low_ref, even_table, odd_table, coef, prof,
    *, step_count,
):
    step = pl.program_id(0)
    group, degrees = link_ref.shape
    north = cos_ref.shape[1]
    local = group * step_count
    half = pair_ref.shape[2] // 2
    done_group = jnp.maximum(step - 1, 0)
    tiles = north // 128
    sweeps = degrees // 128
    orders_each = group // sweeps

    @pl.when(step == 0)
    def _():
        coef[...] = jnp.zeros_like(coef)

    degree = lax.broadcasted_iota(jnp.int32, (group, degrees), 1).astype(jnp.float32)
    link = link_ref[...]
    sign = sign_ref[...]
    for q, ref in enumerate((psi_ref, heat_ref, mag_ref, speed_ref)):
        for c in range(2):
            plain = ref[c, 0]
            sets = [(2 * q + c, plain)]
            if q < 3:
                sets.append((8 + 2 * q + c, plain * degree))
                sets.append((16 + 2 * q + c, pltpu.roll(plain * link, degrees - 1, 1)))
            for row, value in sets:
                signed = value * sign
                for a in range(sweeps):
                    cut = slice(a * 128, (a + 1) * 128)
                    coef[a, pl.ds(row, group, stride=SET_ROWS), :] = value[:, cut]
                    coef[a, pl.ds(SET_ROWS // 2 + row, group, stride=SET_ROWS), :] = signed[:, cut]

    def run(fill, ready):
        cosine = jnp.broadcast_to(cos_ref[...], (group, north))
        wide = jnp.broadcast_to(cos_ref[...], (8, north))
        zero = jnp.zeros((group, north), jnp.float32)

        def one_order(m):
            values = jnp.concatenate(
                [ready[a, pl.ds(m, degrees, stride=group), :] for a in range(tiles)], axis=1
            )
            high, low = halves(values)
            high_ref[m] = high
            low_ref[m] = low
            start = pl.multiple_of(m * SET_ROWS, SET_ROWS)
            rows = jnp.concatenate(
                [coef[a, pl.ds(start, SET_ROWS), :] for a in range(sweeps)], axis=1
            )
            rows_high, rows_low = halves(rows)
            both = dot(jnp.concatenate([rows_high, rows_low], axis=0), high)
            result = both[:SET_ROWS] + both[SET_ROWS:] + dot(rows_high, low)
            pieces = jnp.concatenate(
                [
                    result[0:8],
                    wide * result[8:16] - result[16:24],
                    result[24:32],
                    -wide * result[32:40] - result[40:48],
                ],
                axis=0,
            )
            first = pl.multiple_of((done_group * group + m) * PROFILE_ROWS, PROFILE_ROWS)
            for a in range(tiles):
                prof[a, pl.ds(first, PROFILE_ROWS), :] = pieces[:, a * 128 : (a + 1) * 128]

        def sweep(position, state):
            before, current, log_scale = state
            base = pl.multiple_of(position * 128, 128)
            rise = rise_ref[:, pl.ds(base, 128)]
            fall = fall_ref[:, pl.ds(base, 128)]
            diag = diag_ref[:, pl.ds(base, 128)]
            for part in range(4):
                if part * orders_each % 4 == 0:
                    one_order(position * orders_each + part * orders_each // 4)
                scale = jnp.exp(log_scale)
                for offset in range(32):
                    i = part * 32 + offset
                    fresh = rise[:, i : i + 1] * cosine * current + (
                        diag[:, i : i + 1] - fall[:, i : i + 1] * before
                    )
                    before, current = current, fresh
                    row = fresh * scale
                    start = pl.multiple_of((base + i) * group, group)
                    for a in range(tiles):
                        fill[a, pl.ds(start, group), :] = row[:, a * 128 : (a + 1) * 128]
                magnitude = jnp.maximum(jnp.abs(before), jnp.abs(current))
                magnitude = jnp.where(magnitude > 0.0, magnitude, 1.0)
                before = before / magnitude
                current = current / magnitude
                log_scale = log_scale + jnp.log(magnitude)
            return before, current, log_scale

        lax.fori_loop(0, sweeps, sweep, (zero, zero, log_ref[...]))

    @pl.when(step % 2 == 0)
    def _():
        run(even_table, odd_table)

    @pl.when(step % 2 == 1)
    def _():
        run(odd_table, even_table)

    @pl.when(step == step_count)
    def _():
        places = [2, 4, 0, 8, 10, 12, 6]
        for side in range(2):
            for q, place in enumerate(places):
                target_ref, slot = (pair_ref, q) if q < 2 else (rest_ref, q - 2)
                first = side * 16 + place
                for a in range(tiles):
                    block = jnp.concatenate(
                        [
                            prof[a, pl.ds(first + c, local, stride=PROFILE_ROWS), :]
                            for c in range(2)
                        ],
                        axis=0,
                    )
                    turned = block.T
                    lat = a * 128
                    while lat < (a + 1) * 128:
                        target, offset = divmod(lat, half)
                        count = min(half - offset, (a + 1) * 128 - lat)
                        target_ref[target, slot, pl.ds(side * half + offset, count), :] = turned[
                            lat - a * 128 : lat - a * 128 + count
                        ]
                        lat += count


def synthesis(spectra, link, sign, rise, fall, diag, log_start, cosine, targets):
    local, degrees = link.shape
    north = cosine.shape[1]
    group = 8
    step_count = local // group
    done = lambda g: jnp.maximum(g - 1, 0)
    fresh = lambda g: jnp.minimum(g, step_count - 1)
    spec = pl.BlockSpec((2, 1, group, degrees), lambda g: (0, 0, done(g), 0))
    done_spec = pl.BlockSpec((group, degrees), lambda g: (done(g), 0))
    fresh_spec = pl.BlockSpec((group, degrees), lambda g: (fresh(g), 0))
    legendre_spec = pl.BlockSpec((group, degrees, north), lambda g: (done(g), 0, 0))
    rows = 2 * (north // targets)
    pair_shape = (targets, 2, rows, 2 * local)
    rest_shape = (targets, 5, rows, 2 * local)
    table = pltpu.VMEM((north // 128, group * degrees, 128), jnp.float32)
    return pl.pallas_call(
        functools.partial(synthesis_kernel, step_count=step_count),
        grid=(step_count + 1,),
        in_specs=[spec] * 4
        + [done_spec] * 2
        + [fresh_spec] * 3
        + [
            pl.BlockSpec((group, north), lambda g: (fresh(g), 0)),
            pl.BlockSpec((1, north), lambda g: (0, 0)),
        ],
        out_specs=[
            pl.BlockSpec(pair_shape, lambda g: (0, 0, 0, 0)),
            pl.BlockSpec(rest_shape, lambda g: (0, 0, 0, 0)),
            legendre_spec,
            legendre_spec,
        ],
        out_shape=[
            jax.ShapeDtypeStruct(pair_shape, jnp.float32),
            jax.ShapeDtypeStruct(rest_shape, jnp.float32),
            jax.ShapeDtypeStruct((local, degrees, north), jnp.bfloat16),
            jax.ShapeDtypeStruct((local, degrees, north), jnp.bfloat16),
        ],
        scratch_shapes=[
            table,
            table,
            pltpu.VMEM((degrees // 128, group * SET_ROWS, 128), jnp.float32),
            pltpu.VMEM((north // 128, local * PROFILE_ROWS, 128), jnp.float32),
        ],
        compiler_params=pltpu.CompilerParams(vmem_limit_bytes=VMEM_BYTES),
        cost_estimate=pl.CostEstimate(
            flops=2 * 3 * SET_ROWS * local * degrees * north,
            bytes_accessed=4 * local * degrees * north,
            transcendentals=0,
        ),
        name="synthesis",
    )(*spectra, link, sign, rise, fall, diag, log_start, cosine)


def grid_kernel(
    pair_ref, rest_ref, above_ref, below_ref, weight_ref, spin_ref, high_ref, low_ref, factor_ref,
    out_ref, sets, total, *, step_count, slope_scale, lon_total,
):
    step = pl.program_id(0)
    sources, _, rows, lanes = pair_ref.shape
    count = 9 * rows

    @pl.when(step == 0)
    def _():
        total[...] = jnp.zeros_like(total)
        for source in range(sources):
            cut = slice(source * lanes, (source + 1) * lanes)
            weight = weight_ref[:, cut]
            spin = spin_ref[:, cut]
            for q in range(9):
                if q < 3:
                    plain = pair_ref[source, q - 1] if q else rest_ref[source, 0]
                    value = pltpu.roll(plain, lanes // 2, 1) * spin
                elif q < 7:
                    value = rest_ref[source, q - 2] * weight
                else:
                    value = (above_ref[source, q - 7] - below_ref[source, q - 7]) * (
                        weight * slope_scale
                    )
                high, low = halves(value)
                sets[q * rows : (q + 1) * rows, cut] = high
                sets[count + q * rows : count + (q + 1) * rows, cut] = low

    both = dot(sets[...], high_ref[...])
    grids = both[:count] + both[count:] + dot(sets[:count], low_ref[...])
    g = [grids[q * rows : (q + 1) * rows] for q in range(9)]
    factor = factor_ref[...]
    heat = -((g[3] * g[1] - g[0] * g[4]) * factor + g[6] * g[7])
    induction = -((g[3] * g[2] - g[0] * g[5]) * factor + g[6] * g[8])
    high, low = halves(jnp.concatenate([heat, induction], axis=0))
    back = dot_t(jnp.concatenate([high, low], axis=0), high_ref[...])
    total[...] += back[: 2 * rows] + back[2 * rows :] + dot_t(high, low_ref[...])

    @pl.when(step == step_count - 1)
    def _():
        for source in range(sources):
            cut = slice(source * lanes, (source + 1) * lanes)
            for f in range(2):
                out_ref[source, f] = total[f * rows : (f + 1) * rows, cut] * (1.0 / lon_total)


def grid_step(pair, rest, above, below, weight, spin, wave_high, wave_low, factor, slope_scale):
    sources, _, rows, lanes = pair.shape
    waves, lon_total = wave_high.shape
    lon_block = math.gcd(256, lon_total)
    step_count = lon_total // lon_block
    whole = lambda shape: pl.BlockSpec(shape, lambda i: (0,) * len(shape))
    wave_spec = pl.BlockSpec((waves, lon_block), lambda i: (0, i))
    out_shape = (sources, 2, rows, lanes)
    return pl.pallas_call(
        functools.partial(
            grid_kernel, step_count=step_count, slope_scale=slope_scale, lon_total=lon_total
        ),
        grid=(step_count,),
        in_specs=[
            whole(pair.shape), whole(rest.shape), whole(above.shape), whole(below.shape),
            whole(weight.shape), whole(spin.shape), wave_spec, wave_spec, whole(factor.shape),
        ],
        out_specs=whole(out_shape),
        out_shape=jax.ShapeDtypeStruct(out_shape, jnp.float32),
        scratch_shapes=[
            pltpu.VMEM((18 * rows, waves), jnp.bfloat16),
            pltpu.VMEM((2 * rows, waves), jnp.float32),
        ],
        compiler_params=pltpu.CompilerParams(vmem_limit_bytes=VMEM_BYTES),
        cost_estimate=pl.CostEstimate(
            flops=2 * 3 * 11 * rows * waves * lon_total,
            bytes_accessed=4 * waves * lon_total,
            transcendentals=0,
        ),
        name="grid_step",
    )(pair, rest, above, below, weight, spin, wave_high, wave_low, factor)


def analysis_kernel(
    back_ref, quad_ref, sign_ref, heat_ref, mag_ref, high_ref, low_ref, out_ref,
    values, tend, *, step_count,
):
    step = pl.program_id(0)
    blocks, _, rows, lanes = back_ref.shape
    half = rows // 2
    local = lanes // 2
    group = local // step_count
    north = quad_ref.shape[1]

    @pl.when(step == 0)
    def _():
        for f in range(2):
            sides = []
            for side in range(2):
                stacked = jnp.concatenate(
                    [back_ref[b, f, side * half : (side + 1) * half] for b in range(blocks)], axis=0
                )
                sides.append(stacked.T)
            quad = quad_ref[...]
            for sign, mixed in enumerate((sides[0] + sides[1], sides[0] - sides[1])):
                mixed = mixed * quad
                for c in range(2):
                    row = sign * 4 + f * 2 + c
                    for a in range(north // 128):
                        values[a, pl.ds(row, local, stride=8), :] = mixed[
                            c * local : (c + 1) * local, a * 128 : (a + 1) * 128
                        ]

    def one_order(m, carry):
        start = pl.multiple_of((step * group + m) * 8, 8)
        rows_in = jnp.concatenate(
            [values[a, pl.ds(start, 8), :] for a in range(north // 128)], axis=1
        )
        row_high = rows_in.astype(jnp.bfloat16).astype(jnp.float32)
        row_low = rows_in - row_high
        both = jnp.concatenate([row_high, row_low], axis=0).astype(jnp.bfloat16)
        first = dot_t(both, high_ref[m])
        second = dot_t(both, low_ref[m])
        result = first[:8] + first[8:] + second[:8]
        for a in range(result.shape[1] // 128):
            tend[a, pl.ds(pl.multiple_of(m * 8, 8), 8), :] = result[:, a * 128 : (a + 1) * 128]
        return carry

    lax.fori_loop(0, group, one_order, 0)
    even = sign_ref[...] > 0.0
    for f, ref in enumerate((heat_ref, mag_ref)):
        for c in range(2):
            parts = [
                jnp.concatenate(
                    [
                        tend[a, pl.ds(sign * 4 + f * 2 + c, group, stride=8), :]
                        for a in range(even.shape[1] // 128)
                    ],
                    axis=1,
                )
                for sign in range(2)
            ]
            out_ref[0, f, c] = ref[c, 0] + time_step * jnp.where(even, parts[0], parts[1])


def analysis(back, quad, sign, heat, mag, high, low, step_count):
    local, degrees, north = high.shape
    group = local // step_count
    spec = pl.BlockSpec((2, 1, group, degrees), lambda g: (0, 0, g, 0))
    legendre_spec = pl.BlockSpec((group, degrees, north), lambda g: (g, 0, 0))
    return pl.pallas_call(
        functools.partial(analysis_kernel, step_count=step_count),
        grid=(step_count,),
        in_specs=[
            pl.BlockSpec(back.shape, lambda g: (0, 0, 0, 0)),
            pl.BlockSpec(quad.shape, lambda g: (0, 0)),
            pl.BlockSpec((group, degrees), lambda g: (g, 0)),
            spec, spec, legendre_spec, legendre_spec,
        ],
        out_specs=pl.BlockSpec((1, 2, 2, group, degrees), lambda g: (g, 0, 0, 0, 0)),
        out_shape=jax.ShapeDtypeStruct((step_count, 2, 2, group, degrees), jnp.float32),
        scratch_shapes=[
            pltpu.VMEM((north // 128, local * 8, 128), jnp.float32),
            pltpu.VMEM((degrees // 128, group * 8, 128), jnp.float32),
        ],
        compiler_params=pltpu.CompilerParams(vmem_limit_bytes=VMEM_BYTES),
        cost_estimate=pl.CostEstimate(
            flops=2 * 3 * 8 * local * degrees * north,
            bytes_accessed=4 * local * degrees * north,
            transcendentals=0,
        ),
        name="analysis",
    )(back, quad, sign, heat, mag, high, low)


def wave_halves(orders, lon_total):
    width = 128
    def pair(columns):
        phase_int = orders[:, None] * columns[None, :] % lon_total
        angle_vals = 2.0 * math.pi / lon_total * phase_int.astype(jnp.float32)
        return jnp.cos(angle_vals), jnp.sin(angle_vals)

    fine_cos, fine_sin = pair(jnp.arange(width, dtype=jnp.int32))
    far_cos, far_sin = pair(jnp.arange(lon_total // width, dtype=jnp.int32) * width)
    cos_parts, sin_parts = [], []
    for a in range(lon_total // width):
        ca, sa = far_cos[:, a : a + 1], far_sin[:, a : a + 1]
        cos_parts.append(ca * fine_cos - sa * fine_sin)
        sin_parts.append(-(sa * fine_cos + ca * fine_sin))
    return jnp.concatenate(cos_parts, axis=1), jnp.concatenate(sin_parts, axis=1)


def kernel_body(
    toroidal_stream_spectra,
    thermal_spectra,
    induction_potential,
    outward_speed_spectra,
    position_azimuth_map,
    subdiagonal_complement,
    superdiagonal_complement,
    diagonal_entries,
):
    row_count = lax.axis_size("row")
    ma_count = lax.axis_size("ma")
    local = thermal_spectra.shape[2]
    degrees = thermal_spectra.shape[3]
    north = NLAT // 2
    half = north // ma_count
    spacing = shell_span / row_count

    row_index = lax.axis_index("row")
    slot_start = lax.axis_index("ma") * local
    my_orders = lax.dynamic_slice_in_dim(position_azimuth_map, slot_start, local)
    order_col = my_orders.astype(jnp.float32)[:, None]
    degree = jnp.arange(degrees, dtype=jnp.float32)[None, :]
    degree_ints = jnp.arange(degrees, dtype=jnp.int32)
    even_mask = (my_orders[:, None] + degree_ints[None, :]) % 2 == 0
    sign = jnp.where(even_mask, 1.0, -1.0)
    above_diag = degree > order_col
    square = degree * degree - order_col * order_col
    link = jnp.where(
        above_diag,
        jnp.sqrt(
            jnp.maximum((2.0 * degree + 1.0) * square, 0.0) / jnp.maximum(2.0 * degree - 1.0, 1.0)
        ),
        0.0,
    )
    denominator = jnp.where(above_diag, square, 1.0)
    rise = jnp.where(
        above_diag, jnp.sqrt(jnp.maximum(4.0 * degree * degree - 1.0, 1.0) / denominator), 0.0
    )
    lower_term = (degree - 1.0) * (degree - 1.0) - order_col * order_col
    fall = jnp.where(
        above_diag,
        jnp.sqrt(
            jnp.maximum((2.0 * degree + 1.0) * lower_term, 0.0)
            / (jnp.maximum(2.0 * degree - 3.0, 1.0) * denominator)
        ),
        0.0,
    )
    diag = jnp.where(degree == order_col, 1.0, 0.0)
    theta = math.pi * (jnp.arange(NLAT, dtype=jnp.float32) + 0.5) / NLAT
    cosine = jnp.cos(theta)[None, :north]
    sine = jnp.sin(theta)[None, :north]
    log_start = (
        0.5 * (lax.lgamma(order_col + 1.5) - lax.lgamma(order_col + 1.0) - log_gamma_half)
        - 0.5 * math.log(2.0)
        + order_col * jnp.log(sine)
    )
    pair, rest, high, low = synthesis(
        (toroidal_stream_spectra, thermal_spectra, induction_potential, outward_speed_spectra),
        link, sign, rise, fall, diag, log_start, cosine, ma_count,
    )
    pair = lax.all_to_all(pair, "ma", 0, 0, tiled=True)
    pair, rest = lax.optimization_barrier((pair, rest))
    rest = lax.all_to_all(rest, "ma", 0, 0, tiled=True)

    cos_wave, sin_wave = wave_halves(position_azimuth_map, NLON)
    wave = jnp.stack(
        [cos_wave.reshape(ma_count, local, NLON), sin_wave.reshape(ma_count, local, NLON)], axis=1
    ).reshape(2 * ma_count * local, NLON)
    rounded = lax.reduce_precision(wave, 8, 7)
    wave_high = rounded.astype(jnp.bfloat16)
    wave_low = (wave - rounded).astype(jnp.bfloat16)
    orders = position_azimuth_map.astype(jnp.float32).reshape(ma_count, 1, local)
    weight = jnp.where(orders == 0.0, 1.0, 2.0)
    spin = jnp.concatenate([-orders * weight, orders * weight], axis=1).reshape(1, -1)
    weight = jnp.concatenate([weight, weight], axis=1).reshape(1, -1)

    forward = [(i, i + 1) for i in range(row_count - 1)]
    backward = [(target, source) for source, target in forward]
    below = lax.ppermute(pair, "row", forward)
    above = lax.ppermute(pair, "row", backward)

    lat_index = lax.axis_index("ma") * half + jnp.arange(half, dtype=jnp.int32)
    sine_mine = jnp.sin(math.pi * (lat_index.astype(jnp.float32) + 0.5) / NLAT)
    radius = inner_radius + spacing * (row_index.astype(jnp.float32) + 0.5)
    factor = 1.0 / (radius * radius * (sine_mine * sine_mine))
    factor = jnp.concatenate([factor, factor])[:, None]
    spectra = grid_step(
        pair, rest, above, below, weight, spin, wave_high, wave_low, factor, 1.0 / (2.0 * spacing)
    )
    small = jnp.stack([subdiagonal_complement, superdiagonal_complement, diagonal_entries])
    small, spectra = lax.optimization_barrier((small, spectra))
    factors = jnp.zeros((row_count,) + small.shape, jnp.float32)
    factors = lax.dynamic_update_slice_in_dim(factors, small[None], row_index, 0)
    for shift in range(1, row_count):
        moved = lax.ppermute(
            small, "row", [(i, (i + shift) % row_count) for i in range(row_count)]
        )
        factors = lax.dynamic_update_slice_in_dim(
            factors, moved[None], (row_index + row_count - shift) % row_count, 0
        )
    factors = factors[:, :, :, 0]

    back = lax.all_to_all(spectra, "ma", 0, 0, tiled=True)

    quad = fejer_weights(north, NLAT)[None, :]
    right_side = analysis(
        back, quad, sign, thermal_spectra, induction_potential, high, low, row_count
    )
    shells = lax.all_to_all(right_side, "row", 0, 0, tiled=True)
    spread = lambda k, which: factors[k, which][:, None, None, :]
    running = jnp.zeros_like(shells[0])
    scaled = []
    for k in range(row_count):
        running = shells[k] + (1.0 - spread(k, 0)) * running
        scaled.append(running / spread(k, 2))
    running = jnp.zeros_like(shells[0])
    solved = []
    for k in reversed(range(row_count)):
        running = scaled[k] + (1.0 - spread(k, 1)) * running
        solved.append(running)
    solved = lax.all_to_all(jnp.stack(solved[::-1]), "row", 0, 0, tiled=True)
    solved = jnp.transpose(solved, (1, 2, 0, 3, 4)).reshape(2, 2, 1, local, degrees)
    return solved[0], solved[1]


def program(*args):
    row_count = lax.axis_size("row")
    ma_count = lax.axis_size("ma")
    _, shells, local, degrees = args[1].shape
    fits = (
        shells == 1
        and (NLAT // 2) % (8 * ma_count) == 0
        and (2 * local) % 128 == 0
        and local % (16 * row_count) == 0
        and degrees % 128 == 0
        and 8 % (degrees // 128) == 0
        and (NLAT // 2) % 128 == 0
        and NLON % 128 == 0
    )
    return kernel_body(*args) if fits else body(*args)


def solution(mesh):
    in_specs = (
        P(None, "row", "ma", None),
        P(None, "row", "ma", None),
        P(None, "row", "ma", None),
        P(None, "row", "ma", None),
        P(),
        P(None, "row", None),
        P(None, "row", None),
        P(None, "row", None),
    )
    out_specs = (P(None, "row", "ma", None), P(None, "row", "ma", None))
    return jax.shard_map(program, mesh=mesh, in_specs=in_specs, out_specs=out_specs, check_vma=False)
```

```python
import functools
import math

import jax
import jax.numpy as jnp
from jax import lax
from jax.experimental import pallas as pl
from jax.experimental.pallas import tpu as pltpu
from jax.sharding import PartitionSpec as P

NLAT = 768
NLON = 1536


inner_radius = 0.35
shell_span = 0.65
time_step = 0.001
highest = lax.Precision.HIGHEST
log_gamma_half = 0.5 * math.log(math.pi) - math.log(2.0)


def extended(block, sides, width):
    for axis, dim in sides:
        count = lax.axis_size(axis)
        forward = [(i, i + 1) for i in range(count - 1)]
        backward = [(target, source) for source, target in forward]
        low = lax.ppermute(
            lax.slice_in_dim(block, block.shape[dim] - width, None, axis=dim), axis, forward
        )
        high = lax.ppermute(lax.slice_in_dim(block, 0, width, axis=dim), axis, backward)
        block = jnp.concatenate([low, block, high], axis=dim)
    return block


def entering_2(part, axis, combine, identity, reverse):
    count = lax.axis_size(axis)
    place = lax.axis_index(axis)
    ahead = count - 1 - place if reverse else place
    gathered = jax.tree.map(lambda a: lax.all_gather(a, axis), part)
    state = jax.tree.map(lambda a, e: jnp.zeros_like(a) + jnp.asarray(e, a.dtype), part, identity)

    def one(step, state):
        source = count - 1 - step if reverse else step
        return combine(
            state, jax.tree.map(lambda a: lax.dynamic_index_in_dim(a, source, 0, False), gathered)
        )

    return lax.fori_loop(0, ahead, one, state)


def legendre_rows(orders, cosine, sine_vals, harmonic_index_array):
    block_len = math.gcd(32, harmonic_index_array)
    dtype_ref = cosine.dtype
    order_col = orders[:, None]
    log_start = (
        0.5 * (lax.lgamma(order_col + 1.5) - lax.lgamma(order_col + 1.0) - log_gamma_half)
        - 0.5 * math.log(2.0)
        + order_col * jnp.log(sine_vals)[None, :]
    )
    zero_state = jnp.zeros(log_start.shape, dtype_ref)
    legendre = jnp.zeros((orders.shape[0], harmonic_index_array, cosine.shape[0]), dtype_ref)

    def sweep(position, state_tuple):
        before, current, log_scale, legendre = state_tuple
        new_rows = []
        for offset in range(block_len):
            degree_now = (position * block_len + offset).astype(dtype_ref)
            above_diag = degree_now > order_col
            square = degree_now * degree_now - order_col * order_col
            denominator = jnp.where(above_diag, square, 1.0)
            rise_coef = jnp.where(
                above_diag,
                jnp.sqrt(jnp.maximum(4.0 * degree_now * degree_now - 1.0, 1.0) / denominator),
                0.0,
            )
            lower_term = (degree_now - 1.0) * (degree_now - 1.0) - order_col * order_col
            fall_coef = jnp.where(
                above_diag,
                jnp.sqrt(
                    jnp.maximum((2.0 * degree_now + 1.0) * lower_term, 0.0)
                    / (jnp.maximum(2.0 * degree_now - 3.0, 1.0) * denominator)
                ),
                0.0,
            )
            fresh_row = jnp.where(
                degree_now == order_col,
                1.0,
                rise_coef * cosine[None, :] * current - fall_coef * before,
            )
            before, current = (current, fresh_row)
            new_rows.append(fresh_row * jnp.exp(log_scale))
        magnitude = jnp.maximum(jnp.abs(before), jnp.abs(current))
        magnitude = jnp.where(magnitude > 0.0, magnitude, 1.0)
        before = before / magnitude
        current = current / magnitude
        log_scale = log_scale + jnp.log(magnitude)
        first_row = (position * block_len).astype(jnp.int32)
        legendre = lax.dynamic_update_slice(
            legendre, jnp.stack(new_rows, axis=1), (jnp.int32(0), first_row, jnp.int32(0))
        )
        return (before, current, log_scale, legendre)

    state_tuple = lax.fori_loop(
        0, harmonic_index_array // block_len, sweep, (zero_state, zero_state, log_start, legendre)
    )
    return state_tuple[3]


def wave_table(orders, first_col, column_count, lon_total):
    column_ids = first_col + jnp.arange(column_count, dtype=jnp.int32)
    phase_int = orders[:, None] * column_ids[None, :] % lon_total
    angle_vals = 2.0 * math.pi / lon_total * phase_int.astype(jnp.float32)
    return jnp.stack([jnp.cos(angle_vals), -jnp.sin(angle_vals)], axis=1)


def to_longitudes(spectra, orders, lon_total):
    order_weight = jnp.where(orders == 0, 1.0, 2.0).astype(spectra.dtype)
    weighted = spectra * order_weight[:, None, None, None, None]
    lon_block = math.gcd(512, lon_total)
    output_buf = jnp.zeros(
        (spectra.shape[1], spectra.shape[2], spectra.shape[4], lon_total), spectra.dtype
    )

    def place(position, output_buf):
        first_col = (position * lon_block).astype(jnp.int32)
        wave_block = wave_table(orders, first_col, lon_block, lon_total)
        grid_piece = jnp.einsum("mfscn,mcp->fsnp", weighted, wave_block, precision=highest)
        return lax.dynamic_update_slice(
            output_buf, grid_piece, (jnp.int32(0), jnp.int32(0), jnp.int32(0), first_col)
        )

    return lax.fori_loop(0, lon_total // lon_block, place, output_buf)


def from_longitudes(grid_sets, orders, lon_total):
    lon_block = math.gcd(512, lon_total)
    running_sum = jnp.zeros(
        (orders.shape[0], grid_sets.shape[0], grid_sets.shape[1], 2, grid_sets.shape[2]),
        grid_sets.dtype,
    )

    def add_block(position, running_sum):
        first_col = (position * lon_block).astype(jnp.int32)
        wave_block = wave_table(orders, first_col, lon_block, lon_total)
        grid_piece = lax.dynamic_slice_in_dim(grid_sets, first_col, lon_block, 3)
        return running_sum + jnp.einsum(
            "fsnp,mcp->mfscn", grid_piece, wave_block, precision=highest
        )

    return lax.fori_loop(0, lon_total // lon_block, add_block, running_sum) / lon_total


def fejer_weights(node_count, lat_total):
    term_count = lat_total // 2
    wave_ints = jnp.arange(1, term_count + 1, dtype=jnp.int32)
    node_ints = 2 * jnp.arange(node_count, dtype=jnp.int32) + 1
    phase_int = wave_ints[:, None] * node_ints[None, :] % (2 * lat_total)
    cosines = jnp.cos(math.pi / lat_total * phase_int.astype(jnp.float32))
    wave_vals = wave_ints.astype(jnp.float32)
    ratio_vals = cosines / (4.0 * wave_vals * wave_vals - 1.0)[:, None]
    return 2.0 / lat_total * (1.0 - 2.0 * jnp.sum(ratio_vals, axis=0))


def nonlinear(grid_sets, factor):
    heat_term = -(
        (grid_sets[3] * grid_sets[1] - grid_sets[0] * grid_sets[4]) * factor
        + grid_sets[6] * grid_sets[7]
    )
    field_term = -(
        (grid_sets[3] * grid_sets[2] - grid_sets[0] * grid_sets[5]) * factor
        + grid_sets[6] * grid_sets[8]
    )
    return jnp.stack([heat_term, field_term])


def join_maps(earlier_map, later_map):
    return (
        earlier_map[0] * later_map[0],
        earlier_map[1] * later_map[0][:, None, None, :] + later_map[1],
    )


def body(
    toroidal_stream_spectra,
    thermal_spectra,
    induction_potential,
    outward_speed_spectra,
    position_azimuth_map,
    subdiagonal_complement,
    superdiagonal_complement,
    diagonal_entries,
):
    layer_indices = thermal_spectra.shape[1]
    local_azimuthal_numbers = thermal_spectra.shape[2]
    harmonic_index_array = thermal_spectra.shape[3]
    latitude_rows = NLAT // lax.axis_size("ma")
    north_count = NLAT // 2
    spacing = shell_span / (layer_indices * lax.axis_size("row"))
    slot_start = lax.axis_index("ma") * local_azimuthal_numbers
    my_orders = lax.dynamic_slice_in_dim(position_azimuth_map, slot_start, local_azimuthal_numbers)
    order_float = my_orders.astype(jnp.float32)
    degree_vals = jnp.arange(harmonic_index_array, dtype=jnp.float32)
    degree_ints = jnp.arange(harmonic_index_array, dtype=jnp.int32)
    even_mask = (my_orders[:, None] + degree_ints[None, :]) % 2 == 0
    parity_sign = jnp.where(even_mask, 1.0, -1.0)
    above_diag = degree_vals[None, :] > order_float[:, None]
    link_coef = jnp.where(
        above_diag,
        jnp.sqrt(
            jnp.maximum(
                (2.0 * degree_vals + 1.0)
                * (degree_vals * degree_vals - order_float[:, None] * order_float[:, None]),
                0.0,
            )
            / jnp.maximum(2.0 * degree_vals - 1.0, 1.0)
        ),
        0.0,
    )
    theta_all = math.pi * (jnp.arange(NLAT, dtype=jnp.float32) + 0.5) / NLAT
    cosine_all = jnp.cos(theta_all)
    cosine_north = cosine_all[:north_count]
    sine_north = jnp.sin(theta_all[:north_count])
    weights = fejer_weights(north_count, NLAT)
    legendre_all = legendre_rows(order_float, cosine_north, sine_north, harmonic_index_array)
    coupled_quantities = jnp.stack([thermal_spectra, induction_potential])
    motion_groupings = jnp.stack([toroidal_stream_spectra, thermal_spectra, induction_potential])
    weighted = motion_groupings * degree_vals
    product = motion_groupings * link_coef[None, None, None]
    lifted = jnp.concatenate([product[..., 1:], jnp.zeros_like(product[..., :1])], axis=-1)
    coef_sets = jnp.concatenate(
        [motion_groupings, weighted, lifted, outward_speed_spectra[None]], axis=0
    )
    set_count = 10
    coeffs = jnp.transpose(coef_sets, (3, 0, 2, 1, 4)).reshape(
        local_azimuthal_numbers, set_count * layer_indices * 2, harmonic_index_array
    )
    column_count = coeffs.shape[1]
    stacked = jnp.concatenate([coeffs, coeffs * parity_sign[:, None, :]], axis=1)
    result = jnp.einsum("ocl,oln->ocn", stacked, legendre_all, precision=highest)
    result = jnp.concatenate(
        [result[:, :column_count], jnp.flip(result[:, column_count:], axis=2)], axis=2
    ).reshape(local_azimuthal_numbers, set_count, layer_indices, 2, NLAT)
    plain_part = result[:, 0:3]
    slant_part = cosine_all * result[:, 3:6] - result[:, 6:9]
    outgoing = jnp.concatenate([plain_part, slant_part, result[:, 9:10]], axis=1)
    arrived = lax.all_to_all(outgoing, "ma", split_axis=4, concat_axis=0, tiled=True)
    spin_all = position_azimuth_map.astype(jnp.float32)[:, None, None, None]
    base_part = arrived[:, 0:3]
    turned_all = jnp.stack(
        [-spin_all * base_part[:, :, :, 1], spin_all * base_part[:, :, :, 0]], axis=3
    )
    full_sets = jnp.concatenate([turned_all, arrived[:, 3:7], base_part[:, 1:3]], axis=1)
    grid_sets = to_longitudes(full_sets, position_azimuth_map, NLON)
    padded = extended(grid_sets[7:9], (("row", 1),), 1)
    depthwise_slope = (padded[:, 2:] - padded[:, :-2]) / (2.0 * spacing)
    grid_sets = jnp.concatenate([grid_sets[0:7], depthwise_slope], axis=0)
    lat_index = lax.axis_index("ma") * latitude_rows + jnp.arange(latitude_rows, dtype=jnp.int32)
    theta_mine = math.pi * (lat_index.astype(jnp.float32) + 0.5) / NLAT
    sine_mine = jnp.sin(theta_mine)
    shell_index = lax.axis_index("row") * layer_indices + jnp.arange(layer_indices, dtype=jnp.int32)
    radius = inner_radius + spacing * (shell_index.astype(jnp.float32) + 0.5)
    factor = 1.0 / (radius[:, None] * radius[:, None] * (sine_mine * sine_mine)[None, :])
    forcing = nonlinear(grid_sets, factor[:, :, None])
    spectra = from_longitudes(forcing, position_azimuth_map, NLON)
    returned = lax.all_to_all(spectra, "ma", split_axis=0, concat_axis=4, tiled=True)
    values = returned.reshape(local_azimuthal_numbers, 4 * layer_indices, NLAT)
    column_count = values.shape[1]
    north_part = values[:, :, :north_count]
    south_part = jnp.flip(values[:, :, north_count:], axis=2)
    stacked = jnp.concatenate(
        [(north_part + south_part) * weights, (north_part - south_part) * weights], axis=1
    )
    result = jnp.einsum("ocn,oln->ocl", stacked, legendre_all, precision=highest)
    tendency = jnp.where(even_mask[:, None, :], result[:, :column_count], result[:, column_count:])
    tendency = jnp.transpose(
        tendency.reshape(local_azimuthal_numbers, 2, layer_indices, 2, harmonic_index_array),
        (1, 3, 2, 0, 4),
    )
    right_side = coupled_quantities + time_step * tendency
    keep_low = 1.0 - subdiagonal_complement
    keep_up = 1.0 - superdiagonal_complement
    unit_gains = jnp.ones((2, harmonic_index_array), jnp.float32)
    zero_block = jnp.zeros(right_side[:, :, 0].shape, jnp.float32)
    running_sum = zero_block
    through = unit_gains
    each_shell = 0
    running_sum = (
        right_side[:, :, each_shell] + keep_low[:, each_shell][:, None, None, :] * running_sum
    )
    through = through * keep_low[:, each_shell]
    entering = entering_2(
        (through, running_sum), "row", join_maps, (unit_gains, zero_block), False
    )[1]
    running = entering
    each_shell = 0
    running = right_side[:, :, each_shell] + keep_low[:, each_shell][:, None, None, :] * running
    scaled = [running / diagonal_entries[:, each_shell][:, None, None, :]]
    running_sum = zero_block
    through = unit_gains
    for each_shell in reversed(range(layer_indices)):
        running_sum = scaled[each_shell] + keep_up[:, each_shell][:, None, None, :] * running_sum
        through = through * keep_up[:, each_shell]
    entering = entering_2((through, running_sum), "row", join_maps, (unit_gains, zero_block), True)[
        1
    ]
    running = entering
    results = []
    for each_shell in reversed(range(layer_indices)):
        running = scaled[each_shell] + keep_up[:, each_shell][:, None, None, :] * running
        results.append(running)
    solved = jnp.stack(results[::-1], axis=2)
    return (solved[0], solved[1])


VMEM_BYTES = 60 * 1024 * 1024
SET_ROWS = 48
PROFILE_ROWS = 32


def halves(values):
    high = values.astype(jnp.bfloat16)
    return high, (values - high.astype(jnp.float32)).astype(jnp.bfloat16)


def dot(left, right):
    return jnp.dot(left, right, preferred_element_type=jnp.float32)


def dot_t(left, right):
    return lax.dot_general(
        left, right, (((1,), (1,)), ((), ())), preferred_element_type=jnp.float32
    )


def synthesis_kernel(
    psi_ref, heat_ref, mag_ref, speed_ref, link_ref, sign_ref, rise_ref, fall_ref, diag_ref,
    log_ref, cos_ref, pair_ref, rest_ref, high_ref, low_ref, even_table, odd_table, coef, prof,
    *, step_count,
):
    step = pl.program_id(0)
    group, degrees = link_ref.shape
    north = cos_ref.shape[1]
    local = group * step_count
    half = pair_ref.shape[2] // 2
    done_group = jnp.maximum(step - 1, 0)
    tiles = north // 128
    sweeps = degrees // 128
    orders_each = group // sweeps

    @pl.when(step == 0)
    def _():
        coef[...] = jnp.zeros_like(coef)

    degree = lax.broadcasted_iota(jnp.int32, (group, degrees), 1).astype(jnp.float32)
    link = link_ref[...]
    sign = sign_ref[...]
    for q, ref in enumerate((psi_ref, heat_ref, mag_ref, speed_ref)):
        for c in range(2):
            plain = ref[c, 0]
            sets = [(2 * q + c, plain)]
            if q < 3:
                sets.append((8 + 2 * q + c, plain * degree))
                sets.append((16 + 2 * q + c, pltpu.roll(plain * link, degrees - 1, 1)))
            for row, value in sets:
                signed = value * sign
                for a in range(sweeps):
                    cut = slice(a * 128, (a + 1) * 128)
                    coef[a, pl.ds(row, group, stride=SET_ROWS), :] = value[:, cut]
                    coef[a, pl.ds(SET_ROWS // 2 + row, group, stride=SET_ROWS), :] = signed[:, cut]

    def run(fill, ready):
        cosine = jnp.broadcast_to(cos_ref[...], (group, north))
        wide = jnp.broadcast_to(cos_ref[...], (8, north))
        zero = jnp.zeros((group, north), jnp.float32)

        def one_order(m):
            values = jnp.concatenate(
                [ready[a, pl.ds(m, degrees, stride=group), :] for a in range(tiles)], axis=1
            )
            high, low = halves(values)
            high_ref[m] = high
            low_ref[m] = low
            start = pl.multiple_of(m * SET_ROWS, SET_ROWS)
            rows = jnp.concatenate(
                [coef[a, pl.ds(start, SET_ROWS), :] for a in range(sweeps)], axis=1
            )
            rows_high, rows_low = halves(rows)
            both = dot(jnp.concatenate([rows_high, rows_low], axis=0), high)
            result = both[:SET_ROWS] + both[SET_ROWS:] + dot(rows_high, low)
            pieces = jnp.concatenate(
                [
                    result[0:8],
                    wide * result[8:16] - result[16:24],
                    result[24:32],
                    -wide * result[32:40] - result[40:48],
                ],
                axis=0,
            )
            first = pl.multiple_of((done_group * group + m) * PROFILE_ROWS, PROFILE_ROWS)
            for a in range(tiles):
                prof[a, pl.ds(first, PROFILE_ROWS), :] = pieces[:, a * 128 : (a + 1) * 128]

        def sweep(position, state):
            before, current, log_scale = state
            base = pl.multiple_of(position * 128, 128)
            rise = rise_ref[:, pl.ds(base, 128)]
            fall = fall_ref[:, pl.ds(base, 128)]
            diag = diag_ref[:, pl.ds(base, 128)]
            for part in range(4):
                if part * orders_each % 4 == 0:
                    one_order(position * orders_each + part * orders_each // 4)
                scale = jnp.exp(log_scale)
                for offset in range(32):
                    i = part * 32 + offset
                    fresh = rise[:, i : i + 1] * cosine * current + (
                        diag[:, i : i + 1] - fall[:, i : i + 1] * before
                    )
                    before, current = current, fresh
                    row = fresh * scale
                    start = pl.multiple_of((base + i) * group, group)
                    for a in range(tiles):
                        fill[a, pl.ds(start, group), :] = row[:, a * 128 : (a + 1) * 128]
                magnitude = jnp.maximum(jnp.abs(before), jnp.abs(current))
                magnitude = jnp.where(magnitude > 0.0, magnitude, 1.0)
                before = before / magnitude
                current = current / magnitude
                log_scale = log_scale + jnp.log(magnitude)
            return before, current, log_scale

        lax.fori_loop(0, sweeps, sweep, (zero, zero, log_ref[...]))

    @pl.when(step % 2 == 0)
    def _():
        run(even_table, odd_table)

    @pl.when(step % 2 == 1)
    def _():
        run(odd_table, even_table)

    @pl.when(step == step_count)
    def _():
        places = [2, 4, 0, 8, 10, 12, 6]
        for side in range(2):
            for q, place in enumerate(places):
                target_ref, slot = (pair_ref, q) if q < 2 else (rest_ref, q - 2)
                first = side * 16 + place
                for a in range(tiles):
                    block = jnp.concatenate(
                        [
                            prof[a, pl.ds(first + c, local, stride=PROFILE_ROWS), :]
                            for c in range(2)
                        ],
                        axis=0,
                    )
                    turned = block.T
                    lat = a * 128
                    while lat < (a + 1) * 128:
                        target, offset = divmod(lat, half)
                        count = min(half - offset, (a + 1) * 128 - lat)
                        target_ref[target, slot, pl.ds(side * half + offset, count), :] = turned[
                            lat - a * 128 : lat - a * 128 + count
                        ]
                        lat += count


def synthesis(spectra, link, sign, rise, fall, diag, log_start, cosine, targets):
    local, degrees = link.shape
    north = cosine.shape[1]
    group = 8
    step_count = local // group
    done = lambda g: jnp.maximum(g - 1, 0)
    fresh = lambda g: jnp.minimum(g, step_count - 1)
    spec = pl.BlockSpec((2, 1, group, degrees), lambda g: (0, 0, done(g), 0))
    done_spec = pl.BlockSpec((group, degrees), lambda g: (done(g), 0))
    fresh_spec = pl.BlockSpec((group, degrees), lambda g: (fresh(g), 0))
    legendre_spec = pl.BlockSpec((group, degrees, north), lambda g: (done(g), 0, 0))
    rows = 2 * (north // targets)
    pair_shape = (targets, 2, rows, 2 * local)
    rest_shape = (targets, 5, rows, 2 * local)
    table = pltpu.VMEM((north // 128, group * degrees, 128), jnp.float32)
    return pl.pallas_call(
        functools.partial(synthesis_kernel, step_count=step_count),
        grid=(step_count + 1,),
        in_specs=[spec] * 4
        + [done_spec] * 2
        + [fresh_spec] * 3
        + [
            pl.BlockSpec((group, north), lambda g: (fresh(g), 0)),
            pl.BlockSpec((1, north), lambda g: (0, 0)),
        ],
        out_specs=[
            pl.BlockSpec(pair_shape, lambda g: (0, 0, 0, 0)),
            pl.BlockSpec(rest_shape, lambda g: (0, 0, 0, 0)),
            legendre_spec,
            legendre_spec,
        ],
        out_shape=[
            jax.ShapeDtypeStruct(pair_shape, jnp.float32),
            jax.ShapeDtypeStruct(rest_shape, jnp.float32),
            jax.ShapeDtypeStruct((local, degrees, north), jnp.bfloat16),
            jax.ShapeDtypeStruct((local, degrees, north), jnp.bfloat16),
        ],
        scratch_shapes=[
            table,
            table,
            pltpu.VMEM((degrees // 128, group * SET_ROWS, 128), jnp.float32),
            pltpu.VMEM((north // 128, local * PROFILE_ROWS, 128), jnp.float32),
        ],
        compiler_params=pltpu.CompilerParams(vmem_limit_bytes=VMEM_BYTES),
        cost_estimate=pl.CostEstimate(
            flops=2 * 3 * SET_ROWS * local * degrees * north,
            bytes_accessed=4 * local * degrees * north,
            transcendentals=0,
        ),
        name="synthesis",
    )(*spectra, link, sign, rise, fall, diag, log_start, cosine)


def grid_kernel(
    pair_ref, rest_ref, above_ref, below_ref, weight_ref, spin_ref, near_ref, far_ref, factor_ref,
    out_ref, sets, total, *, step_count, slope_scale, lon_total,
):
    step = pl.program_id(0)
    sources, _, rows, lanes = pair_ref.shape
    count = 9 * rows

    @pl.when(step == 0)
    def _():
        total[...] = jnp.zeros_like(total)
        for source in range(sources):
            cut = slice(source * lanes, (source + 1) * lanes)
            weight = weight_ref[:, cut]
            spin = spin_ref[:, cut]
            for q in range(9):
                if q < 3:
                    plain = pair_ref[source, q - 1] if q else rest_ref[source, 0]
                    value = pltpu.roll(plain, lanes // 2, 1) * spin
                elif q < 7:
                    value = rest_ref[source, q - 2] * weight
                else:
                    value = (above_ref[source, q - 7] - below_ref[source, q - 7]) * (
                        weight * slope_scale
                    )
                high, low = halves(value)
                sets[q * rows : (q + 1) * rows, cut] = high
                sets[count + q * rows : count + (q + 1) * rows, cut] = low

    pieces = [
        far_ref[0, :, 2 * a : 2 * a + 1] * near_ref[0]
        + far_ref[0, :, 2 * a + 1 : 2 * a + 2] * near_ref[1]
        for a in range(far_ref.shape[2] // 2)
    ]
    wave_high, wave_low = halves(jnp.concatenate(pieces, axis=1))
    both = dot(sets[...], wave_high)
    grids = both[:count] + both[count:] + dot(sets[:count], wave_low)
    g = [grids[q * rows : (q + 1) * rows] for q in range(9)]
    factor = factor_ref[...]
    heat = -((g[3] * g[1] - g[0] * g[4]) * factor + g[6] * g[7])
    induction = -((g[3] * g[2] - g[0] * g[5]) * factor + g[6] * g[8])
    high, low = halves(jnp.concatenate([heat, induction], axis=0))
    back = dot_t(jnp.concatenate([high, low], axis=0), wave_high)
    total[...] += back[: 2 * rows] + back[2 * rows :] + dot_t(high, wave_low)

    @pl.when(step == step_count - 1)
    def _():
        for source in range(sources):
            cut = slice(source * lanes, (source + 1) * lanes)
            for f in range(2):
                out_ref[source, f] = total[f * rows : (f + 1) * rows, cut] * (1.0 / lon_total)


def grid_step(pair, rest, above, below, weight, spin, near, far, factor, slope_scale, lon_total):
    sources, _, rows, lanes = pair.shape
    step_count, waves, _ = far.shape
    whole = lambda shape: pl.BlockSpec(shape, lambda i: (0,) * len(shape))
    far_spec = pl.BlockSpec((1, waves, far.shape[2]), lambda i: (i, 0, 0))
    out_shape = (sources, 2, rows, lanes)
    return pl.pallas_call(
        functools.partial(
            grid_kernel, step_count=step_count, slope_scale=slope_scale, lon_total=lon_total
        ),
        grid=(step_count,),
        in_specs=[
            whole(pair.shape), whole(rest.shape), whole(above.shape), whole(below.shape),
            whole(weight.shape), whole(spin.shape), whole(near.shape), far_spec, whole(factor.shape),
        ],
        out_specs=whole(out_shape),
        out_shape=jax.ShapeDtypeStruct(out_shape, jnp.float32),
        scratch_shapes=[
            pltpu.VMEM((18 * rows, waves), jnp.bfloat16),
            pltpu.VMEM((2 * rows, waves), jnp.float32),
        ],
        compiler_params=pltpu.CompilerParams(vmem_limit_bytes=VMEM_BYTES),
        cost_estimate=pl.CostEstimate(
            flops=2 * 3 * 11 * rows * waves * lon_total,
            bytes_accessed=4 * waves * lon_total,
            transcendentals=0,
        ),
        name="grid_step",
    )(pair, rest, above, below, weight, spin, near, far, factor)


def analysis_kernel(
    back_ref, quad_ref, sign_ref, heat_ref, mag_ref, high_ref, low_ref, out_ref,
    values, tend, *, step_count,
):
    step = pl.program_id(0)
    blocks, _, rows, lanes = back_ref.shape
    half = rows // 2
    local = lanes // 2
    group = local // step_count
    north = quad_ref.shape[1]

    @pl.when(step == 0)
    def _():
        for f in range(2):
            sides = []
            for side in range(2):
                stacked = jnp.concatenate(
                    [back_ref[b, f, side * half : (side + 1) * half] for b in range(blocks)], axis=0
                )
                sides.append(stacked.T)
            quad = quad_ref[...]
            for sign, mixed in enumerate((sides[0] + sides[1], sides[0] - sides[1])):
                mixed = mixed * quad
                for c in range(2):
                    row = sign * 4 + f * 2 + c
                    for a in range(north // 128):
                        values[a, pl.ds(row, local, stride=8), :] = mixed[
                            c * local : (c + 1) * local, a * 128 : (a + 1) * 128
                        ]

    def one_order(m, carry):
        start = pl.multiple_of((step * group + m) * 8, 8)
        rows_in = jnp.concatenate(
            [values[a, pl.ds(start, 8), :] for a in range(north // 128)], axis=1
        )
        row_high = rows_in.astype(jnp.bfloat16).astype(jnp.float32)
        row_low = rows_in - row_high
        both = jnp.concatenate([row_high, row_low], axis=0).astype(jnp.bfloat16)
        first = dot_t(both, high_ref[m])
        second = dot_t(both, low_ref[m])
        result = first[:8] + first[8:] + second[:8]
        for a in range(result.shape[1] // 128):
            tend[a, pl.ds(pl.multiple_of(m * 8, 8), 8), :] = result[:, a * 128 : (a + 1) * 128]
        return carry

    lax.fori_loop(0, group, one_order, 0)
    even = sign_ref[...] > 0.0
    for f, ref in enumerate((heat_ref, mag_ref)):
        for c in range(2):
            parts = [
                jnp.concatenate(
                    [
                        tend[a, pl.ds(sign * 4 + f * 2 + c, group, stride=8), :]
                        for a in range(even.shape[1] // 128)
                    ],
                    axis=1,
                )
                for sign in range(2)
            ]
            out_ref[0, f, c] = ref[c, 0] + time_step * jnp.where(even, parts[0], parts[1])


def analysis(back, quad, sign, heat, mag, high, low, step_count):
    local, degrees, north = high.shape
    group = local // step_count
    spec = pl.BlockSpec((2, 1, group, degrees), lambda g: (0, 0, g, 0))
    legendre_spec = pl.BlockSpec((group, degrees, north), lambda g: (g, 0, 0))
    return pl.pallas_call(
        functools.partial(analysis_kernel, step_count=step_count),
        grid=(step_count,),
        in_specs=[
            pl.BlockSpec(back.shape, lambda g: (0, 0, 0, 0)),
            pl.BlockSpec(quad.shape, lambda g: (0, 0)),
            pl.BlockSpec((group, degrees), lambda g: (g, 0)),
            spec, spec, legendre_spec, legendre_spec,
        ],
        out_specs=pl.BlockSpec((1, 2, 2, group, degrees), lambda g: (g, 0, 0, 0, 0)),
        out_shape=jax.ShapeDtypeStruct((step_count, 2, 2, group, degrees), jnp.float32),
        scratch_shapes=[
            pltpu.VMEM((north // 128, local * 8, 128), jnp.float32),
            pltpu.VMEM((degrees // 128, group * 8, 128), jnp.float32),
        ],
        compiler_params=pltpu.CompilerParams(vmem_limit_bytes=VMEM_BYTES),
        cost_estimate=pl.CostEstimate(
            flops=2 * 3 * 8 * local * degrees * north,
            bytes_accessed=4 * local * degrees * north,
            transcendentals=0,
        ),
        name="analysis",
    )(back, quad, sign, heat, mag, high, low)


def wave_factors(orders, lon_total):
    width = 128

    def pair(columns):
        phase_int = orders[:, None] * columns[None, :] % lon_total
        angle_vals = 2.0 * math.pi / lon_total * phase_int.astype(jnp.float32)
        return jnp.cos(angle_vals), jnp.sin(angle_vals)

    near = pair(jnp.arange(width, dtype=jnp.int32))
    far = pair(jnp.arange(lon_total // width, dtype=jnp.int32) * width)
    return near, far


def kernel_body(
    toroidal_stream_spectra,
    thermal_spectra,
    induction_potential,
    outward_speed_spectra,
    position_azimuth_map,
    subdiagonal_complement,
    superdiagonal_complement,
    diagonal_entries,
):
    row_count = lax.axis_size("row")
    ma_count = lax.axis_size("ma")
    local = thermal_spectra.shape[2]
    degrees = thermal_spectra.shape[3]
    north = NLAT // 2
    half = north // ma_count
    spacing = shell_span / row_count

    row_index = lax.axis_index("row")
    slot_start = lax.axis_index("ma") * local
    my_orders = lax.dynamic_slice_in_dim(position_azimuth_map, slot_start, local)
    order_col = my_orders.astype(jnp.float32)[:, None]
    degree = jnp.arange(degrees, dtype=jnp.float32)[None, :]
    degree_ints = jnp.arange(degrees, dtype=jnp.int32)
    even_mask = (my_orders[:, None] + degree_ints[None, :]) % 2 == 0
    sign = jnp.where(even_mask, 1.0, -1.0)
    above_diag = degree > order_col
    square = degree * degree - order_col * order_col
    link = jnp.where(
        above_diag,
        jnp.sqrt(
            jnp.maximum((2.0 * degree + 1.0) * square, 0.0) / jnp.maximum(2.0 * degree - 1.0, 1.0)
        ),
        0.0,
    )
    denominator = jnp.where(above_diag, square, 1.0)
    rise = jnp.where(
        above_diag, jnp.sqrt(jnp.maximum(4.0 * degree * degree - 1.0, 1.0) / denominator), 0.0
    )
    lower_term = (degree - 1.0) * (degree - 1.0) - order_col * order_col
    fall = jnp.where(
        above_diag,
        jnp.sqrt(
            jnp.maximum((2.0 * degree + 1.0) * lower_term, 0.0)
            / (jnp.maximum(2.0 * degree - 3.0, 1.0) * denominator)
        ),
        0.0,
    )
    diag = jnp.where(degree == order_col, 1.0, 0.0)
    theta = math.pi * (jnp.arange(NLAT, dtype=jnp.float32) + 0.5) / NLAT
    cosine = jnp.cos(theta)[None, :north]
    sine = jnp.sin(theta)[None, :north]
    log_start = (
        0.5 * (lax.lgamma(order_col + 1.5) - lax.lgamma(order_col + 1.0) - log_gamma_half)
        - 0.5 * math.log(2.0)
        + order_col * jnp.log(sine)
    )
    pair, rest, high, low = synthesis(
        (toroidal_stream_spectra, thermal_spectra, induction_potential, outward_speed_spectra),
        link, sign, rise, fall, diag, log_start, cosine, ma_count,
    )
    pair = lax.all_to_all(pair, "ma", 0, 0, tiled=True)
    pair, rest = lax.optimization_barrier((pair, rest))
    rest = lax.all_to_all(rest, "ma", 0, 0, tiled=True)

    (near_cos, near_sin), (far_cos, far_sin) = wave_factors(position_azimuth_map, NLON)
    chunk = math.gcd(2, far_cos.shape[1])

    def by_component(first, second):
        parts = [v.reshape(ma_count, local, v.shape[1]) for v in (first, second)]
        return jnp.stack(parts, axis=1).reshape(2 * ma_count * local, first.shape[1])

    near = jnp.stack([by_component(near_cos, near_cos), by_component(near_sin, near_sin)])
    far = jnp.stack([by_component(far_cos, -far_sin), by_component(-far_sin, -far_cos)], axis=2)
    far = jnp.moveaxis(far.reshape(far.shape[0], -1, 2 * chunk), 1, 0)
    orders = position_azimuth_map.astype(jnp.float32).reshape(ma_count, 1, local)
    weight = jnp.where(orders == 0.0, 1.0, 2.0)
    spin = jnp.concatenate([-orders * weight, orders * weight], axis=1).reshape(1, -1)
    weight = jnp.concatenate([weight, weight], axis=1).reshape(1, -1)

    forward = [(i, i + 1) for i in range(row_count - 1)]
    backward = [(target, source) for source, target in forward]
    below = lax.ppermute(pair, "row", forward)
    above = lax.ppermute(pair, "row", backward)

    lat_index = lax.axis_index("ma") * half + jnp.arange(half, dtype=jnp.int32)
    sine_mine = jnp.sin(math.pi * (lat_index.astype(jnp.float32) + 0.5) / NLAT)
    radius = inner_radius + spacing * (row_index.astype(jnp.float32) + 0.5)
    factor = 1.0 / (radius * radius * (sine_mine * sine_mine))
    factor = jnp.concatenate([factor, factor])[:, None]
    spectra = grid_step(
        pair, rest, above, below, weight, spin, near, far, factor, 1.0 / (2.0 * spacing), NLON
    )
    small = jnp.stack([subdiagonal_complement, superdiagonal_complement, diagonal_entries])
    small, spectra = lax.optimization_barrier((small, spectra))
    factors = jnp.zeros((row_count,) + small.shape, jnp.float32)
    factors = lax.dynamic_update_slice_in_dim(factors, small[None], row_index, 0)
    for shift in range(1, row_count):
        moved = lax.ppermute(
            small, "row", [(i, (i + shift) % row_count) for i in range(row_count)]
        )
        factors = lax.dynamic_update_slice_in_dim(
            factors, moved[None], (row_index + row_count - shift) % row_count, 0
        )
    factors = factors[:, :, :, 0]

    back = lax.all_to_all(spectra, "ma", 0, 0, tiled=True)

    quad = fejer_weights(north, NLAT)[None, :]
    right_side = analysis(
        back, quad, sign, thermal_spectra, induction_potential, high, low, row_count
    )
    shells = lax.all_to_all(right_side, "row", 0, 0, tiled=True)
    spread = lambda k, which: factors[k, which][:, None, None, :]
    running = jnp.zeros_like(shells[0])
    scaled = []
    for k in range(row_count):
        running = shells[k] + (1.0 - spread(k, 0)) * running
        scaled.append(running / spread(k, 2))
    running = jnp.zeros_like(shells[0])
    solved = []
    for k in reversed(range(row_count)):
        running = scaled[k] + (1.0 - spread(k, 1)) * running
        solved.append(running)
    solved = lax.all_to_all(jnp.stack(solved[::-1]), "row", 0, 0, tiled=True)
    solved = jnp.transpose(solved, (1, 2, 0, 3, 4)).reshape(2, 2, 1, local, degrees)
    return solved[0], solved[1]


def program(*args):
    row_count = lax.axis_size("row")
    ma_count = lax.axis_size("ma")
    _, shells, local, degrees = args[1].shape
    fits = (
        shells == 1
        and (NLAT // 2) % (8 * ma_count) == 0
        and (2 * local) % 128 == 0
        and local % (16 * row_count) == 0
        and degrees % 128 == 0
        and 8 % (degrees // 128) == 0
        and (NLAT // 2) % 128 == 0
        and NLON % 128 == 0
    )
    return kernel_body(*args) if fits else body(*args)


def solution(mesh):
    in_specs = (
        P(None, "row", "ma", None),
        P(None, "row", "ma", None),
        P(None, "row", "ma", None),
        P(None, "row", "ma", None),
        P(),
        P(None, "row", None),
        P(None, "row", None),
        P(None, "row", None),
    )
    out_specs = (P(None, "row", "ma", None), P(None, "row", "ma", None))
    return jax.shard_map(program, mesh=mesh, in_specs=in_specs, out_specs=out_specs, check_vma=False)
```

```python
import functools
import math

import jax
import jax.numpy as jnp
from jax import lax
from jax.experimental import pallas as pl
from jax.experimental.pallas import tpu as pltpu
from jax.sharding import PartitionSpec as P

NLAT = 768
NLON = 1536


inner_radius = 0.35
shell_span = 0.65
time_step = 0.001
highest = lax.Precision.HIGHEST
log_gamma_half = 0.5 * math.log(math.pi) - math.log(2.0)


def extended(block, sides, width):
    for axis, dim in sides:
        count = lax.axis_size(axis)
        forward = [(i, i + 1) for i in range(count - 1)]
        backward = [(target, source) for source, target in forward]
        low = lax.ppermute(
            lax.slice_in_dim(block, block.shape[dim] - width, None, axis=dim), axis, forward
        )
        high = lax.ppermute(lax.slice_in_dim(block, 0, width, axis=dim), axis, backward)
        block = jnp.concatenate([low, block, high], axis=dim)
    return block


def entering_2(part, axis, combine, identity, reverse):
    count = lax.axis_size(axis)
    place = lax.axis_index(axis)
    ahead = count - 1 - place if reverse else place
    gathered = jax.tree.map(lambda a: lax.all_gather(a, axis), part)
    state = jax.tree.map(lambda a, e: jnp.zeros_like(a) + jnp.asarray(e, a.dtype), part, identity)

    def one(step, state):
        source = count - 1 - step if reverse else step
        return combine(
            state, jax.tree.map(lambda a: lax.dynamic_index_in_dim(a, source, 0, False), gathered)
        )

    return lax.fori_loop(0, ahead, one, state)


def legendre_rows(orders, cosine, sine_vals, harmonic_index_array):
    block_len = math.gcd(32, harmonic_index_array)
    dtype_ref = cosine.dtype
    order_col = orders[:, None]
    log_start = (
        0.5 * (lax.lgamma(order_col + 1.5) - lax.lgamma(order_col + 1.0) - log_gamma_half)
        - 0.5 * math.log(2.0)
        + order_col * jnp.log(sine_vals)[None, :]
    )
    zero_state = jnp.zeros(log_start.shape, dtype_ref)
    legendre = jnp.zeros((orders.shape[0], harmonic_index_array, cosine.shape[0]), dtype_ref)

    def sweep(position, state_tuple):
        before, current, log_scale, legendre = state_tuple
        new_rows = []
        for offset in range(block_len):
            degree_now = (position * block_len + offset).astype(dtype_ref)
            above_diag = degree_now > order_col
            square = degree_now * degree_now - order_col * order_col
            denominator = jnp.where(above_diag, square, 1.0)
            rise_coef = jnp.where(
                above_diag,
                jnp.sqrt(jnp.maximum(4.0 * degree_now * degree_now - 1.0, 1.0) / denominator),
                0.0,
            )
            lower_term = (degree_now - 1.0) * (degree_now - 1.0) - order_col * order_col
            fall_coef = jnp.where(
                above_diag,
                jnp.sqrt(
                    jnp.maximum((2.0 * degree_now + 1.0) * lower_term, 0.0)
                    / (jnp.maximum(2.0 * degree_now - 3.0, 1.0) * denominator)
                ),
                0.0,
            )
            fresh_row = jnp.where(
                degree_now == order_col,
                1.0,
                rise_coef * cosine[None, :] * current - fall_coef * before,
            )
            before, current = (current, fresh_row)
            new_rows.append(fresh_row * jnp.exp(log_scale))
        magnitude = jnp.maximum(jnp.abs(before), jnp.abs(current))
        magnitude = jnp.where(magnitude > 0.0, magnitude, 1.0)
        before = before / magnitude
        current = current / magnitude
        log_scale = log_scale + jnp.log(magnitude)
        first_row = (position * block_len).astype(jnp.int32)
        legendre = lax.dynamic_update_slice(
            legendre, jnp.stack(new_rows, axis=1), (jnp.int32(0), first_row, jnp.int32(0))
        )
        return (before, current, log_scale, legendre)

    state_tuple = lax.fori_loop(
        0, harmonic_index_array // block_len, sweep, (zero_state, zero_state, log_start, legendre)
    )
    return state_tuple[3]


def wave_table(orders, first_col, column_count, lon_total):
    column_ids = first_col + jnp.arange(column_count, dtype=jnp.int32)
    phase_int = orders[:, None] * column_ids[None, :] % lon_total
    angle_vals = 2.0 * math.pi / lon_total * phase_int.astype(jnp.float32)
    return jnp.stack([jnp.cos(angle_vals), -jnp.sin(angle_vals)], axis=1)


def to_longitudes(spectra, orders, lon_total):
    order_weight = jnp.where(orders == 0, 1.0, 2.0).astype(spectra.dtype)
    weighted = spectra * order_weight[:, None, None, None, None]
    lon_block = math.gcd(512, lon_total)
    output_buf = jnp.zeros(
        (spectra.shape[1], spectra.shape[2], spectra.shape[4], lon_total), spectra.dtype
    )

    def place(position, output_buf):
        first_col = (position * lon_block).astype(jnp.int32)
        wave_block = wave_table(orders, first_col, lon_block, lon_total)
        grid_piece = jnp.einsum("mfscn,mcp->fsnp", weighted, wave_block, precision=highest)
        return lax.dynamic_update_slice(
            output_buf, grid_piece, (jnp.int32(0), jnp.int32(0), jnp.int32(0), first_col)
        )

    return lax.fori_loop(0, lon_total // lon_block, place, output_buf)


def from_longitudes(grid_sets, orders, lon_total):
    lon_block = math.gcd(512, lon_total)
    running_sum = jnp.zeros(
        (orders.shape[0], grid_sets.shape[0], grid_sets.shape[1], 2, grid_sets.shape[2]),
        grid_sets.dtype,
    )

    def add_block(position, running_sum):
        first_col = (position * lon_block).astype(jnp.int32)
        wave_block = wave_table(orders, first_col, lon_block, lon_total)
        grid_piece = lax.dynamic_slice_in_dim(grid_sets, first_col, lon_block, 3)
        return running_sum + jnp.einsum(
            "fsnp,mcp->mfscn", grid_piece, wave_block, precision=highest
        )

    return lax.fori_loop(0, lon_total // lon_block, add_block, running_sum) / lon_total


def fejer_weights(node_count, lat_total):
    term_count = lat_total // 2
    wave_ints = jnp.arange(1, term_count + 1, dtype=jnp.int32)
    node_ints = 2 * jnp.arange(node_count, dtype=jnp.int32) + 1
    phase_int = wave_ints[:, None] * node_ints[None, :] % (2 * lat_total)
    cosines = jnp.cos(math.pi / lat_total * phase_int.astype(jnp.float32))
    wave_vals = wave_ints.astype(jnp.float32)
    ratio_vals = cosines / (4.0 * wave_vals * wave_vals - 1.0)[:, None]
    return 2.0 / lat_total * (1.0 - 2.0 * jnp.sum(ratio_vals, axis=0))


def nonlinear(grid_sets, factor):
    heat_term = -(
        (grid_sets[3] * grid_sets[1] - grid_sets[0] * grid_sets[4]) * factor
        + grid_sets[6] * grid_sets[7]
    )
    field_term = -(
        (grid_sets[3] * grid_sets[2] - grid_sets[0] * grid_sets[5]) * factor
        + grid_sets[6] * grid_sets[8]
    )
    return jnp.stack([heat_term, field_term])


def join_maps(earlier_map, later_map):
    return (
        earlier_map[0] * later_map[0],
        earlier_map[1] * later_map[0][:, None, None, :] + later_map[1],
    )


def body(
    toroidal_stream_spectra,
    thermal_spectra,
    induction_potential,
    outward_speed_spectra,
    position_azimuth_map,
    subdiagonal_complement,
    superdiagonal_complement,
    diagonal_entries,
):
    layer_indices = thermal_spectra.shape[1]
    local_azimuthal_numbers = thermal_spectra.shape[2]
    harmonic_index_array = thermal_spectra.shape[3]
    latitude_rows = NLAT // lax.axis_size("ma")
    north_count = NLAT // 2
    spacing = shell_span / (layer_indices * lax.axis_size("row"))
    slot_start = lax.axis_index("ma") * local_azimuthal_numbers
    my_orders = lax.dynamic_slice_in_dim(position_azimuth_map, slot_start, local_azimuthal_numbers)
    order_float = my_orders.astype(jnp.float32)
    degree_vals = jnp.arange(harmonic_index_array, dtype=jnp.float32)
    degree_ints = jnp.arange(harmonic_index_array, dtype=jnp.int32)
    even_mask = (my_orders[:, None] + degree_ints[None, :]) % 2 == 0
    parity_sign = jnp.where(even_mask, 1.0, -1.0)
    above_diag = degree_vals[None, :] > order_float[:, None]
    link_coef = jnp.where(
        above_diag,
        jnp.sqrt(
            jnp.maximum(
                (2.0 * degree_vals + 1.0)
                * (degree_vals * degree_vals - order_float[:, None] * order_float[:, None]),
                0.0,
            )
            / jnp.maximum(2.0 * degree_vals - 1.0, 1.0)
        ),
        0.0,
    )
    theta_all = math.pi * (jnp.arange(NLAT, dtype=jnp.float32) + 0.5) / NLAT
    cosine_all = jnp.cos(theta_all)
    cosine_north = cosine_all[:north_count]
    sine_north = jnp.sin(theta_all[:north_count])
    weights = fejer_weights(north_count, NLAT)
    legendre_all = legendre_rows(order_float, cosine_north, sine_north, harmonic_index_array)
    coupled_quantities = jnp.stack([thermal_spectra, induction_potential])
    motion_groupings = jnp.stack([toroidal_stream_spectra, thermal_spectra, induction_potential])
    weighted = motion_groupings * degree_vals
    product = motion_groupings * link_coef[None, None, None]
    lifted = jnp.concatenate([product[..., 1:], jnp.zeros_like(product[..., :1])], axis=-1)
    coef_sets = jnp.concatenate(
        [motion_groupings, weighted, lifted, outward_speed_spectra[None]], axis=0
    )
    set_count = 10
    coeffs = jnp.transpose(coef_sets, (3, 0, 2, 1, 4)).reshape(
        local_azimuthal_numbers, set_count * layer_indices * 2, harmonic_index_array
    )
    column_count = coeffs.shape[1]
    stacked = jnp.concatenate([coeffs, coeffs * parity_sign[:, None, :]], axis=1)
    result = jnp.einsum("ocl,oln->ocn", stacked, legendre_all, precision=highest)
    result = jnp.concatenate(
        [result[:, :column_count], jnp.flip(result[:, column_count:], axis=2)], axis=2
    ).reshape(local_azimuthal_numbers, set_count, layer_indices, 2, NLAT)
    plain_part = result[:, 0:3]
    slant_part = cosine_all * result[:, 3:6] - result[:, 6:9]
    outgoing = jnp.concatenate([plain_part, slant_part, result[:, 9:10]], axis=1)
    arrived = lax.all_to_all(outgoing, "ma", split_axis=4, concat_axis=0, tiled=True)
    spin_all = position_azimuth_map.astype(jnp.float32)[:, None, None, None]
    base_part = arrived[:, 0:3]
    turned_all = jnp.stack(
        [-spin_all * base_part[:, :, :, 1], spin_all * base_part[:, :, :, 0]], axis=3
    )
    full_sets = jnp.concatenate([turned_all, arrived[:, 3:7], base_part[:, 1:3]], axis=1)
    grid_sets = to_longitudes(full_sets, position_azimuth_map, NLON)
    padded = extended(grid_sets[7:9], (("row", 1),), 1)
    depthwise_slope = (padded[:, 2:] - padded[:, :-2]) / (2.0 * spacing)
    grid_sets = jnp.concatenate([grid_sets[0:7], depthwise_slope], axis=0)
    lat_index = lax.axis_index("ma") * latitude_rows + jnp.arange(latitude_rows, dtype=jnp.int32)
    theta_mine = math.pi * (lat_index.astype(jnp.float32) + 0.5) / NLAT
    sine_mine = jnp.sin(theta_mine)
    shell_index = lax.axis_index("row") * layer_indices + jnp.arange(layer_indices, dtype=jnp.int32)
    radius = inner_radius + spacing * (shell_index.astype(jnp.float32) + 0.5)
    factor = 1.0 / (radius[:, None] * radius[:, None] * (sine_mine * sine_mine)[None, :])
    forcing = nonlinear(grid_sets, factor[:, :, None])
    spectra = from_longitudes(forcing, position_azimuth_map, NLON)
    returned = lax.all_to_all(spectra, "ma", split_axis=0, concat_axis=4, tiled=True)
    values = returned.reshape(local_azimuthal_numbers, 4 * layer_indices, NLAT)
    column_count = values.shape[1]
    north_part = values[:, :, :north_count]
    south_part = jnp.flip(values[:, :, north_count:], axis=2)
    stacked = jnp.concatenate(
        [(north_part + south_part) * weights, (north_part - south_part) * weights], axis=1
    )
    result = jnp.einsum("ocn,oln->ocl", stacked, legendre_all, precision=highest)
    tendency = jnp.where(even_mask[:, None, :], result[:, :column_count], result[:, column_count:])
    tendency = jnp.transpose(
        tendency.reshape(local_azimuthal_numbers, 2, layer_indices, 2, harmonic_index_array),
        (1, 3, 2, 0, 4),
    )
    right_side = coupled_quantities + time_step * tendency
    keep_low = 1.0 - subdiagonal_complement
    keep_up = 1.0 - superdiagonal_complement
    unit_gains = jnp.ones((2, harmonic_index_array), jnp.float32)
    zero_block = jnp.zeros(right_side[:, :, 0].shape, jnp.float32)
    running_sum = zero_block
    through = unit_gains
    each_shell = 0
    running_sum = (
        right_side[:, :, each_shell] + keep_low[:, each_shell][:, None, None, :] * running_sum
    )
    through = through * keep_low[:, each_shell]
    entering = entering_2(
        (through, running_sum), "row", join_maps, (unit_gains, zero_block), False
    )[1]
    running = entering
    each_shell = 0
    running = right_side[:, :, each_shell] + keep_low[:, each_shell][:, None, None, :] * running
    scaled = [running / diagonal_entries[:, each_shell][:, None, None, :]]
    running_sum = zero_block
    through = unit_gains
    for each_shell in reversed(range(layer_indices)):
        running_sum = scaled[each_shell] + keep_up[:, each_shell][:, None, None, :] * running_sum
        through = through * keep_up[:, each_shell]
    entering = entering_2((through, running_sum), "row", join_maps, (unit_gains, zero_block), True)[
        1
    ]
    running = entering
    results = []
    for each_shell in reversed(range(layer_indices)):
        running = scaled[each_shell] + keep_up[:, each_shell][:, None, None, :] * running
        results.append(running)
    solved = jnp.stack(results[::-1], axis=2)
    return (solved[0], solved[1])


VMEM_BYTES = 60 * 1024 * 1024
SET_ROWS = 48
PROFILE_ROWS = 32


def halves(values):
    high = values.astype(jnp.bfloat16)
    return high, (values - high.astype(jnp.float32)).astype(jnp.bfloat16)


def dot(left, right):
    return jnp.dot(left, right, preferred_element_type=jnp.float32)


def dot_t(left, right):
    return lax.dot_general(
        left, right, (((1,), (1,)), ((), ())), preferred_element_type=jnp.float32
    )


def synthesis_kernel(
    psi_ref, heat_ref, mag_ref, speed_ref, link_ref, sign_ref, rise_ref, fall_ref, diag_ref,
    log_ref, cos_ref, pair_ref, rest_ref, high_ref, low_ref, even_table, odd_table, coef, prof,
    *, step_count,
):
    step = pl.program_id(0)
    group, degrees = link_ref.shape
    north = cos_ref.shape[1]
    local = group * step_count
    half = pair_ref.shape[2] // 2
    done_group = jnp.maximum(step - 1, 0)
    tiles = north // 128
    sweeps = degrees // 128
    orders_each = group // sweeps

    @pl.when(step == 0)
    def _():
        coef[...] = jnp.zeros_like(coef)

    degree = lax.broadcasted_iota(jnp.int32, (group, degrees), 1).astype(jnp.float32)
    link = link_ref[...]
    sign = sign_ref[...]
    for q, ref in enumerate((psi_ref, heat_ref, mag_ref, speed_ref)):
        for c in range(2):
            plain = ref[c, 0]
            sets = [(2 * q + c, plain)]
            if q < 3:
                sets.append((8 + 2 * q + c, plain * degree))
                sets.append((16 + 2 * q + c, pltpu.roll(plain * link, degrees - 1, 1)))
            for row, value in sets:
                signed = value * sign
                for a in range(sweeps):
                    cut = slice(a * 128, (a + 1) * 128)
                    coef[a, pl.ds(row, group, stride=SET_ROWS), :] = value[:, cut]
                    coef[a, pl.ds(SET_ROWS // 2 + row, group, stride=SET_ROWS), :] = signed[:, cut]

    def run(fill, ready):
        cosine = jnp.broadcast_to(cos_ref[...], (group, north))
        wide = jnp.broadcast_to(cos_ref[...], (8, north))
        zero = jnp.zeros((group, north), jnp.float32)

        def one_order(m):
            values = jnp.concatenate(
                [ready[a, pl.ds(m, degrees, stride=group), :] for a in range(tiles)], axis=1
            )
            high, low = halves(values)
            high_ref[m] = high
            low_ref[m] = low
            start = pl.multiple_of(m * SET_ROWS, SET_ROWS)
            rows = jnp.concatenate(
                [coef[a, pl.ds(start, SET_ROWS), :] for a in range(sweeps)], axis=1
            )
            rows_high, rows_low = halves(rows)
            both = dot(jnp.concatenate([rows_high, rows_low], axis=0), high)
            result = both[:SET_ROWS] + both[SET_ROWS:] + dot(rows_high, low)
            pieces = jnp.concatenate(
                [
                    result[0:8],
                    wide * result[8:16] - result[16:24],
                    result[24:32],
                    -wide * result[32:40] - result[40:48],
                ],
                axis=0,
            )
            first = pl.multiple_of((done_group * group + m) * PROFILE_ROWS, PROFILE_ROWS)
            for a in range(tiles):
                prof[a, pl.ds(first, PROFILE_ROWS), :] = pieces[:, a * 128 : (a + 1) * 128]

        def sweep(position, state):
            before, current, log_scale = state
            base = pl.multiple_of(position * 128, 128)
            rise = rise_ref[:, pl.ds(base, 128)]
            fall = fall_ref[:, pl.ds(base, 128)]
            diag = diag_ref[:, pl.ds(base, 128)]
            for part in range(4):
                if part * orders_each % 4 == 0:
                    one_order(position * orders_each + part * orders_each // 4)
                scale = jnp.exp(log_scale)
                for offset in range(32):
                    i = part * 32 + offset
                    fresh = rise[:, i : i + 1] * cosine * current + (
                        diag[:, i : i + 1] - fall[:, i : i + 1] * before
                    )
                    before, current = current, fresh
                    row = fresh * scale
                    start = pl.multiple_of((base + i) * group, group)
                    for a in range(tiles):
                        fill[a, pl.ds(start, group), :] = row[:, a * 128 : (a + 1) * 128]
                magnitude = jnp.maximum(jnp.abs(before), jnp.abs(current))
                magnitude = jnp.where(magnitude > 0.0, magnitude, 1.0)
                before = before / magnitude
                current = current / magnitude
                log_scale = log_scale + jnp.log(magnitude)
            return before, current, log_scale

        lax.fori_loop(0, sweeps, sweep, (zero, zero, log_ref[...]))

    @pl.when(step % 2 == 0)
    def _():
        run(even_table, odd_table)

    @pl.when(step % 2 == 1)
    def _():
        run(odd_table, even_table)

    @pl.when(step == step_count)
    def _():
        places = [2, 4, 0, 8, 10, 12, 6]
        for side in range(2):
            for q, place in enumerate(places):
                target_ref, slot = (pair_ref, q) if q < 2 else (rest_ref, q - 2)
                first = side * 16 + place
                for a in range(tiles):
                    block = jnp.concatenate(
                        [
                            prof[a, pl.ds(first + c, local, stride=PROFILE_ROWS), :]
                            for c in range(2)
                        ],
                        axis=0,
                    )
                    turned = block.T
                    lat = a * 128
                    while lat < (a + 1) * 128:
                        target, offset = divmod(lat, half)
                        count = min(half - offset, (a + 1) * 128 - lat)
                        target_ref[target, slot, pl.ds(side * half + offset, count), :] = turned[
                            lat - a * 128 : lat - a * 128 + count
                        ]
                        lat += count


def synthesis(spectra, link, sign, rise, fall, diag, log_start, cosine, targets):
    local, degrees = link.shape
    north = cosine.shape[1]
    group = 8
    step_count = local // group
    done = lambda g: jnp.maximum(g - 1, 0)
    fresh = lambda g: jnp.minimum(g, step_count - 1)
    spec = pl.BlockSpec((2, 1, group, degrees), lambda g: (0, 0, done(g), 0))
    done_spec = pl.BlockSpec((group, degrees), lambda g: (done(g), 0))
    fresh_spec = pl.BlockSpec((group, degrees), lambda g: (fresh(g), 0))
    legendre_spec = pl.BlockSpec((group, degrees, north), lambda g: (done(g), 0, 0))
    rows = 2 * (north // targets)
    pair_shape = (targets, 2, rows, 2 * local)
    rest_shape = (targets, 5, rows, 2 * local)
    table = pltpu.VMEM((north // 128, group * degrees, 128), jnp.float32)
    return pl.pallas_call(
        functools.partial(synthesis_kernel, step_count=step_count),
        grid=(step_count + 1,),
        in_specs=[spec] * 4
        + [done_spec] * 2
        + [fresh_spec] * 3
        + [
            pl.BlockSpec((group, north), lambda g: (fresh(g), 0)),
            pl.BlockSpec((1, north), lambda g: (0, 0)),
        ],
        out_specs=[
            pl.BlockSpec(pair_shape, lambda g: (0, 0, 0, 0)),
            pl.BlockSpec(rest_shape, lambda g: (0, 0, 0, 0)),
            legendre_spec,
            legendre_spec,
        ],
        out_shape=[
            jax.ShapeDtypeStruct(pair_shape, jnp.float32),
            jax.ShapeDtypeStruct(rest_shape, jnp.float32),
            jax.ShapeDtypeStruct((local, degrees, north), jnp.bfloat16),
            jax.ShapeDtypeStruct((local, degrees, north), jnp.bfloat16),
        ],
        scratch_shapes=[
            table,
            table,
            pltpu.VMEM((degrees // 128, group * SET_ROWS, 128), jnp.float32),
            pltpu.VMEM((north // 128, local * PROFILE_ROWS, 128), jnp.float32),
        ],
        compiler_params=pltpu.CompilerParams(vmem_limit_bytes=VMEM_BYTES),
        cost_estimate=pl.CostEstimate(
            flops=2 * 3 * SET_ROWS * local * degrees * north,
            bytes_accessed=4 * local * degrees * north,
            transcendentals=0,
        ),
        name="synthesis",
    )(*spectra, link, sign, rise, fall, diag, log_start, cosine)


def grid_kernel(
    pair_ref, rest_ref, above_ref, below_ref, weight_ref, spin_ref, near_ref, far_ref, factor_ref,
    out_ref, sets, total, *, step_count, slope_scale, lon_total,
):
    step = pl.program_id(0)
    sources, _, rows, lanes = pair_ref.shape
    count = 9 * rows

    @pl.when(step == 0)
    def _():
        total[...] = jnp.zeros_like(total)
        for source in range(sources):
            cut = slice(source * lanes, (source + 1) * lanes)
            weight = weight_ref[:, cut]
            spin = spin_ref[:, cut]
            for q in range(9):
                if q < 3:
                    plain = pair_ref[source, q - 1] if q else rest_ref[source, 0]
                    value = pltpu.roll(plain, lanes // 2, 1) * spin
                elif q < 7:
                    value = rest_ref[source, q - 2] * weight
                else:
                    value = (above_ref[source, q - 7] - below_ref[source, q - 7]) * (
                        weight * slope_scale
                    )
                high, low = halves(value)
                sets[q * rows : (q + 1) * rows, cut] = high
                sets[count + q * rows : count + (q + 1) * rows, cut] = low

    pieces = [
        far_ref[0, :, 2 * a : 2 * a + 1] * near_ref[0]
        + far_ref[0, :, 2 * a + 1 : 2 * a + 2] * near_ref[1]
        for a in range(far_ref.shape[2] // 2)
    ]
    wave_high, wave_low = halves(jnp.concatenate(pieces, axis=1))
    both = dot(sets[...], wave_high)
    grids = both[:count] + both[count:] + dot(sets[:count], wave_low)
    g = [grids[q * rows : (q + 1) * rows] for q in range(9)]
    factor = factor_ref[...]
    heat = -((g[3] * g[1] - g[0] * g[4]) * factor + g[6] * g[7])
    induction = -((g[3] * g[2] - g[0] * g[5]) * factor + g[6] * g[8])
    high, low = halves(jnp.concatenate([heat, induction], axis=0))
    back = dot_t(jnp.concatenate([high, low], axis=0), wave_high)
    total[...] += back[: 2 * rows] + back[2 * rows :] + dot_t(high, wave_low)

    @pl.when(step == step_count - 1)
    def _():
        for source in range(sources):
            cut = slice(source * lanes, (source + 1) * lanes)
            for f in range(2):
                out_ref[source, f] = total[f * rows : (f + 1) * rows, cut] * (1.0 / lon_total)


def grid_step(pair, rest, above, below, weight, spin, near, far, factor, slope_scale, lon_total):
    sources, _, rows, lanes = pair.shape
    step_count, waves, _ = far.shape
    whole = lambda shape: pl.BlockSpec(shape, lambda i: (0,) * len(shape))
    far_spec = pl.BlockSpec((1, waves, far.shape[2]), lambda i: (i, 0, 0))
    out_shape = (sources, 2, rows, lanes)
    return pl.pallas_call(
        functools.partial(
            grid_kernel, step_count=step_count, slope_scale=slope_scale, lon_total=lon_total
        ),
        grid=(step_count,),
        in_specs=[
            whole(pair.shape), whole(rest.shape), whole(above.shape), whole(below.shape),
            whole(weight.shape), whole(spin.shape), whole(near.shape), far_spec, whole(factor.shape),
        ],
        out_specs=whole(out_shape),
        out_shape=jax.ShapeDtypeStruct(out_shape, jnp.float32),
        scratch_shapes=[
            pltpu.VMEM((18 * rows, waves), jnp.bfloat16),
            pltpu.VMEM((2 * rows, waves), jnp.float32),
        ],
        compiler_params=pltpu.CompilerParams(vmem_limit_bytes=VMEM_BYTES),
        cost_estimate=pl.CostEstimate(
            flops=2 * 3 * 11 * rows * waves * lon_total,
            bytes_accessed=4 * waves * lon_total,
            transcendentals=0,
        ),
        name="grid_step",
    )(pair, rest, above, below, weight, spin, near, far, factor)


def analysis_kernel(
    back_ref, quad_ref, sign_ref, heat_ref, mag_ref, high_ref, low_ref, factors_ref,
    new_heat_ref, new_mag_ref, values, tend, shells, send_sems, recv_sems, *, step_count,
):
    step = pl.program_id(0)
    me = lax.axis_index("row")

    def send(position, shift):
        return pltpu.make_async_remote_copy(
            src_ref=shells.at[me, position],
            dst_ref=shells.at[me, position],
            send_sem=send_sems.at[shift - 1, position],
            recv_sem=recv_sems.at[shift - 1, position],
            device_id={"row": lax.rem(me + shift, step_count)},
            device_id_type=pl.DeviceIdType.MESH,
        )

    @pl.when(step == 0)
    def _():
        barrier = pltpu.get_barrier_semaphore()
        for shift in range(1, step_count):
            pl.semaphore_signal(
                barrier,
                inc=1,
                device_id={"row": lax.rem(me + shift, step_count)},
                device_id_type=pl.DeviceIdType.MESH,
            )
        pl.semaphore_wait(barrier, step_count - 1)

    blocks, _, rows, lanes = back_ref.shape
    half = rows // 2
    local = lanes // 2
    group = local // step_count
    north = quad_ref.shape[1]

    @pl.when(step == 0)
    def _():
        for f in range(2):
            sides = []
            for side in range(2):
                stacked = jnp.concatenate(
                    [back_ref[b, f, side * half : (side + 1) * half] for b in range(blocks)], axis=0
                )
                sides.append(stacked.T)
            quad = quad_ref[...]
            for sign, mixed in enumerate((sides[0] + sides[1], sides[0] - sides[1])):
                mixed = mixed * quad
                for c in range(2):
                    row = sign * 4 + f * 2 + c
                    for a in range(north // 128):
                        values[a, pl.ds(row, local, stride=8), :] = mixed[
                            c * local : (c + 1) * local, a * 128 : (a + 1) * 128
                        ]

    def one_order(m, carry):
        start = pl.multiple_of((step * group + m) * 8, 8)
        rows_in = jnp.concatenate(
            [values[a, pl.ds(start, 8), :] for a in range(north // 128)], axis=1
        )
        row_high = rows_in.astype(jnp.bfloat16).astype(jnp.float32)
        row_low = rows_in - row_high
        both = jnp.concatenate([row_high, row_low], axis=0).astype(jnp.bfloat16)
        first = dot_t(both, high_ref[m])
        second = dot_t(both, low_ref[m])
        result = first[:8] + first[8:] + second[:8]
        for a in range(result.shape[1] // 128):
            tend[a, pl.ds(pl.multiple_of(m * 8, 8), 8), :] = result[:, a * 128 : (a + 1) * 128]
        return carry

    lax.fori_loop(0, group, one_order, 0)
    even = sign_ref[...] > 0.0
    for f, ref in enumerate((heat_ref, mag_ref)):
        for c in range(2):
            parts = [
                jnp.concatenate(
                    [
                        tend[a, pl.ds(sign * 4 + f * 2 + c, group, stride=8), :]
                        for a in range(even.shape[1] // 128)
                    ],
                    axis=1,
                )
                for sign in range(2)
            ]
            shells[me, step, f, c] = ref[c, 0] + time_step * jnp.where(even, parts[0], parts[1])
    for shift in range(1, step_count):
        send(step, shift).start()

    @pl.when(step == step_count - 1)
    def _():
        for position in range(step_count):
            for shift in range(1, step_count):
                send(position, shift).wait()
        for f, ref in enumerate((new_heat_ref, new_mag_ref)):
            for position in range(step_count):
                for c in range(2):
                    running = jnp.zeros(shells.shape[-2:], jnp.float32)
                    scaled = []
                    for k in range(step_count):
                        keep = 1.0 - factors_ref[k, 0, f : f + 1]
                        running = shells[k, position, f, c] + keep * running
                        scaled.append(running / factors_ref[k, 2, f : f + 1])
                    running = jnp.zeros_like(running)
                    mine = running
                    for k in reversed(range(step_count)):
                        keep = 1.0 - factors_ref[k, 1, f : f + 1]
                        running = scaled[k] + keep * running
                        mine = jnp.where(me == k, running, mine)
                    ref[c, 0, position * group : (position + 1) * group] = mine


def analysis(back, quad, sign, heat, mag, high, low, factors, step_count):
    local, degrees, north = high.shape
    group = local // step_count
    spec = pl.BlockSpec((2, 1, group, degrees), lambda g: (0, 0, g, 0))
    legendre_spec = pl.BlockSpec((group, degrees, north), lambda g: (g, 0, 0))
    return pl.pallas_call(
        functools.partial(analysis_kernel, step_count=step_count),
        grid=(step_count,),
        in_specs=[
            pl.BlockSpec(back.shape, lambda g: (0, 0, 0, 0)),
            pl.BlockSpec(quad.shape, lambda g: (0, 0)),
            pl.BlockSpec((group, degrees), lambda g: (g, 0)),
            spec, spec, legendre_spec, legendre_spec,
            pl.BlockSpec(factors.shape, lambda g: (0, 0, 0, 0)),
        ],
        out_specs=[pl.BlockSpec(heat.shape, lambda g: (0, 0, 0, 0))] * 2,
        out_shape=[jax.ShapeDtypeStruct(heat.shape, jnp.float32)] * 2,
        scratch_shapes=[
            pltpu.VMEM((north // 128, local * 8, 128), jnp.float32),
            pltpu.VMEM((degrees // 128, group * 8, 128), jnp.float32),
            pltpu.VMEM((step_count, step_count, 2, 2, group, degrees), jnp.float32),
            pltpu.SemaphoreType.DMA((step_count - 1, step_count)),
            pltpu.SemaphoreType.DMA((step_count - 1, step_count)),
        ],
        compiler_params=pltpu.CompilerParams(
            vmem_limit_bytes=VMEM_BYTES, collective_id=0, has_side_effects=True
        ),
        cost_estimate=pl.CostEstimate(
            flops=2 * 3 * 8 * local * degrees * north,
            bytes_accessed=4 * local * degrees * north,
            transcendentals=0,
        ),
        name="analysis",
    )(back, quad, sign, heat, mag, high, low, factors)


def wave_factors(orders, lon_total):
    width = 128

    def pair(columns):
        phase_int = orders[:, None] * columns[None, :] % lon_total
        angle_vals = 2.0 * math.pi / lon_total * phase_int.astype(jnp.float32)
        return jnp.cos(angle_vals), jnp.sin(angle_vals)

    near = pair(jnp.arange(width, dtype=jnp.int32))
    far = pair(jnp.arange(lon_total // width, dtype=jnp.int32) * width)
    return near, far


def kernel_body(
    toroidal_stream_spectra,
    thermal_spectra,
    induction_potential,
    outward_speed_spectra,
    position_azimuth_map,
    subdiagonal_complement,
    superdiagonal_complement,
    diagonal_entries,
):
    row_count = lax.axis_size("row")
    ma_count = lax.axis_size("ma")
    local = thermal_spectra.shape[2]
    degrees = thermal_spectra.shape[3]
    north = NLAT // 2
    half = north // ma_count
    spacing = shell_span / row_count

    row_index = lax.axis_index("row")
    slot_start = lax.axis_index("ma") * local
    my_orders = lax.dynamic_slice_in_dim(position_azimuth_map, slot_start, local)
    order_col = my_orders.astype(jnp.float32)[:, None]
    degree = jnp.arange(degrees, dtype=jnp.float32)[None, :]
    degree_ints = jnp.arange(degrees, dtype=jnp.int32)
    even_mask = (my_orders[:, None] + degree_ints[None, :]) % 2 == 0
    sign = jnp.where(even_mask, 1.0, -1.0)
    above_diag = degree > order_col
    square = degree * degree - order_col * order_col
    link = jnp.where(
        above_diag,
        jnp.sqrt(
            jnp.maximum((2.0 * degree + 1.0) * square, 0.0) / jnp.maximum(2.0 * degree - 1.0, 1.0)
        ),
        0.0,
    )
    denominator = jnp.where(above_diag, square, 1.0)
    rise = jnp.where(
        above_diag, jnp.sqrt(jnp.maximum(4.0 * degree * degree - 1.0, 1.0) / denominator), 0.0
    )
    lower_term = (degree - 1.0) * (degree - 1.0) - order_col * order_col
    fall = jnp.where(
        above_diag,
        jnp.sqrt(
            jnp.maximum((2.0 * degree + 1.0) * lower_term, 0.0)
            / (jnp.maximum(2.0 * degree - 3.0, 1.0) * denominator)
        ),
        0.0,
    )
    diag = jnp.where(degree == order_col, 1.0, 0.0)
    theta = math.pi * (jnp.arange(NLAT, dtype=jnp.float32) + 0.5) / NLAT
    cosine = jnp.cos(theta)[None, :north]
    sine = jnp.sin(theta)[None, :north]
    log_start = (
        0.5 * (lax.lgamma(order_col + 1.5) - lax.lgamma(order_col + 1.0) - log_gamma_half)
        - 0.5 * math.log(2.0)
        + order_col * jnp.log(sine)
    )
    pair, rest, high, low = synthesis(
        (toroidal_stream_spectra, thermal_spectra, induction_potential, outward_speed_spectra),
        link, sign, rise, fall, diag, log_start, cosine, ma_count,
    )
    pair = lax.all_to_all(pair, "ma", 0, 0, tiled=True)
    pair, rest = lax.optimization_barrier((pair, rest))
    rest = lax.all_to_all(rest, "ma", 0, 0, tiled=True)

    (near_cos, near_sin), (far_cos, far_sin) = wave_factors(position_azimuth_map, NLON)
    chunk = math.gcd(2, far_cos.shape[1])

    def by_component(first, second):
        parts = [v.reshape(ma_count, local, v.shape[1]) for v in (first, second)]
        return jnp.stack(parts, axis=1).reshape(2 * ma_count * local, first.shape[1])

    near = jnp.stack([by_component(near_cos, near_cos), by_component(near_sin, near_sin)])
    far = jnp.stack([by_component(far_cos, -far_sin), by_component(-far_sin, -far_cos)], axis=2)
    far = jnp.moveaxis(far.reshape(far.shape[0], -1, 2 * chunk), 1, 0)
    orders = position_azimuth_map.astype(jnp.float32).reshape(ma_count, 1, local)
    weight = jnp.where(orders == 0.0, 1.0, 2.0)
    spin = jnp.concatenate([-orders * weight, orders * weight], axis=1).reshape(1, -1)
    weight = jnp.concatenate([weight, weight], axis=1).reshape(1, -1)

    forward = [(i, i + 1) for i in range(row_count - 1)]
    backward = [(target, source) for source, target in forward]
    below = lax.ppermute(pair, "row", forward)
    above = lax.ppermute(pair, "row", backward)

    lat_index = lax.axis_index("ma") * half + jnp.arange(half, dtype=jnp.int32)
    sine_mine = jnp.sin(math.pi * (lat_index.astype(jnp.float32) + 0.5) / NLAT)
    radius = inner_radius + spacing * (row_index.astype(jnp.float32) + 0.5)
    factor = 1.0 / (radius * radius * (sine_mine * sine_mine))
    factor = jnp.concatenate([factor, factor])[:, None]
    spectra = grid_step(
        pair, rest, above, below, weight, spin, near, far, factor, 1.0 / (2.0 * spacing), NLON
    )
    small = jnp.stack([subdiagonal_complement, superdiagonal_complement, diagonal_entries])
    small, spectra = lax.optimization_barrier((small, spectra))
    factors = jnp.zeros((row_count,) + small.shape, jnp.float32)
    factors = lax.dynamic_update_slice_in_dim(factors, small[None], row_index, 0)
    for shift in range(1, row_count):
        moved = lax.ppermute(
            small, "row", [(i, (i + shift) % row_count) for i in range(row_count)]
        )
        factors = lax.dynamic_update_slice_in_dim(
            factors, moved[None], (row_index + row_count - shift) % row_count, 0
        )
    factors = factors[:, :, :, 0]

    back = lax.all_to_all(spectra, "ma", 0, 0, tiled=True)

    quad = fejer_weights(north, NLAT)[None, :]
    new_heat, new_mag = analysis(
        back, quad, sign, thermal_spectra, induction_potential, high, low, factors, row_count
    )
    return new_heat, new_mag


def program(*args):
    row_count = lax.axis_size("row")
    ma_count = lax.axis_size("ma")
    _, shells, local, degrees = args[1].shape
    fits = (
        shells == 1
        and row_count > 1
        and (NLAT // 2) % (8 * ma_count) == 0
        and (2 * local) % 128 == 0
        and local % (16 * row_count) == 0
        and degrees % 128 == 0
        and 8 % (degrees // 128) == 0
        and (NLAT // 2) % 128 == 0
        and NLON % 128 == 0
    )
    return kernel_body(*args) if fits else body(*args)


def solution(mesh):
    in_specs = (
        P(None, "row", "ma", None),
        P(None, "row", "ma", None),
        P(None, "row", "ma", None),
        P(None, "row", "ma", None),
        P(),
        P(None, "row", None),
        P(None, "row", None),
        P(None, "row", None),
    )
    out_specs = (P(None, "row", "ma", None), P(None, "row", "ma", None))
    return jax.shard_map(program, mesh=mesh, in_specs=in_specs, out_specs=out_specs, check_vma=False)
```
